128 devices in a mesh: seq: 16 (over y, x_lo, core), head: 8 (over x_hi, z).
Axes of the slice: x: 4 (x_hi: 2, x_lo: 2; x = x_hi * 2 + x_lo), y: 4, z: 4, core: 2. Of those that a mesh axis runs over, the one named last changes fastest.
Arguments:
- q_prompt: bfloat16 [2048, 8192], P('seq', 'head'), may hold values from -200 to 200
- k_prompt: bfloat16 [2048, 1024], P('seq', 'head'), may hold values from -6 to 6
- v_prompt: bfloat16 [2048, 1024], P('seq', 'head'), may hold values from -6 to 6
- do_prompt: bfloat16 [2048, 8192], P('seq', 'head'), may hold values from -6 to 6
- q_resp: bfloat16 [4096, 8192], P('seq', 'head'), may hold values from -200 to 200
- k_resp: bfloat16 [4096, 1024], P('seq', 'head'), may hold values from -6 to 6
- v_resp: bfloat16 [4096, 1024], P('seq', 'head'), may hold values from -6 to 6
- do_resp: bfloat16 [4096, 8192], P('seq', 'head'), may hold values from -6 to 6
- resp_lengths: int32 [16, 4], P('seq'), may hold values from 1 to 128, 256 in all within a row
- resp_prompt: int32 [16, 4], P('seq'), may hold values from 0 to 1
- w_query: bfloat16 [5120, 8192], P(None, 'head'), may hold values from -0.75 to 0.75
- w_key: bfloat16 [5120, 1024], P(None, 'head'), may hold values from -0.5 to 0.5
- w_value: bfloat16 [5120, 1024], P(None, 'head'), may hold values from -0.5 to 0.5
Outputs:
- dx_prompt: bfloat16 [2048, 5120], P('seq', 'head')
- dx_resp: bfloat16 [4096, 5120], P('seq', 'head')
The draws below stay inside these ranges and needn't reach their ends.
Inputs may be any that keep to these rules, and one draw needn't show every extreme that they name: `resp_lengths`: each row sums to 256; its largest entry is 128.
All inputs are finite; a program needn't handle non-finite values.
Results may differ from the reference program's by a relative error of at most 0.024.
Values may be sent and summed in bfloat16 or wider, within the bound.
A program may use at most 128 MiB of HBM per device.

```python
import math
import jax
import jax.numpy as jnp
import numpy as np
from jax import lax

D = 5120
HEADS = 64
KV_HEADS = 8
HEAD_DIM = 128
PROMPTS = 2
RESP_DEV = 256
RESP_COUNT = 4
MOST_LEN = 128
PROMPT_ROWS = 2048
PROMPT_LEN = 1024
RESP_ROWS = 4096
N_SEQ = 16
N_HEAD = 8


def shared_keys(key, marker, rows):
    return jax.random.normal(jax.random.fold_in(key, marker), (rows, KV_HEADS, HEAD_DIM), jnp.float32)


def keys_from(key, marker, rows):
    base = jnp.clip(shared_keys(key, marker, rows), -6.0, 6.0)
    return base.reshape(rows, KV_HEADS * HEAD_DIM)


def queries_from(key, own, rows):
    group = HEADS // KV_HEADS
    values = jnp.clip(jax.random.normal(own, (rows, KV_HEADS, group, HEAD_DIM), jnp.float32), -6.0, 6.0)
    return values.reshape(rows, HEADS * HEAD_DIM)


def draw_k_prompt(key, part):
    return keys_from(key, 101, PROMPT_ROWS).astype(jnp.bfloat16)


def draw_q_prompt(key, part):
    own = jax.random.fold_in(key, 7)
    return queries_from(key, own, PROMPT_ROWS).astype(jnp.bfloat16)


def draw_k_resp(key, part):
    return keys_from(key, 202, RESP_ROWS).astype(jnp.bfloat16)


def draw_q_resp(key, part):
    own = jax.random.fold_in(key, 9)
    return queries_from(key, own, RESP_ROWS).astype(jnp.bfloat16)


def plant(array, own_key, least, largest):
    spot = [jax.random.randint(jax.random.fold_in(own_key, axis), (), 0, length) for axis, length in enumerate(array.shape)]
    widest = array.shape.index(max(array.shape))
    neighbour = spot[:widest] + [(spot[widest] + 1) % array.shape[widest]] + spot[widest + 1:]
    return array.at[tuple(spot)].set(least).at[tuple(neighbour)].set(largest)


def strengthened(values, stream_key, source, target, shards_of, factor):
    owner, partner = [(jnp.arange(values.shape[axis_at]) // (values.shape[axis_at] // shards_of)).reshape([-1 if axis == axis_at else 1 for axis in range(values.ndim)]) for axis_at in (source, target)]
    chosen = jax.random.permutation(stream_key, shards_of)[partner]
    strong = (owner == chosen) | (owner == (partner + shards_of // 2) % shards_of)
    return jnp.where(strong, factor * values, values)


def level_of(rng, shape, cuts, low, high):
    def one(axis_at, shards_of):
        steps = jax.random.uniform(jax.random.fold_in(jax.random.fold_in(rng, 6), axis_at), (shards_of,), jnp.float32, low / len(cuts), high / len(cuts))
        return jnp.repeat(jnp.exp(steps), shape[axis_at] // shards_of).reshape((-1,) + (1,) * (len(shape) - axis_at - 1))

    loudness = one(*cuts[0])
    for cut in cuts[1:]:
        loudness = loudness * one(*cut)
    return loudness


def split_up(amount, total, reach, slope):
    weights = [(1 << 20) // math.isqrt(standing ** slope) + 1 for standing in range(2, amount + 1)]
    spare, given = total - reach - (amount - 1), [1] * (amount - 1)
    while spare > 0:
        movable = [i for i in range(amount - 1) if given[i] < reach]
        pool, remaining = sum([weights[i] for i in movable]), spare
        for i in movable:
            extra = min(reach - given[i], max(1, remaining * weights[i] // pool), spare)
            given[i] = given[i] + extra
            spare = spare - extra
    return np.array([reach] + given)


def uneven_parts(own_key, count, total, reach, lean):
    if count == 2:
        one = jax.random.randint(own_key, (), max(1, total - reach), min(reach, total - 1) + 1)
        return jnp.stack([one, total - one])
    sizes = jnp.asarray(split_up(count, total, reach, lean), jnp.int32)
    pairs = (count - 1) // 2
    donor, receiver = sizes[1:1 + 2 * pairs:2], sizes[2:2 + 2 * pairs:2]
    margin = jnp.minimum(donor - 1, reach - receiver)
    shifted = jax.random.randint(jax.random.fold_in(own_key, 1), (pairs,), 0, 1 << 20) % (margin + 1)
    sizes = sizes.at[1:1 + 2 * pairs:2].set(donor - shifted).at[2:2 + 2 * pairs:2].set(receiver + shifted)
    return sizes[jax.random.permutation(jax.random.fold_in(own_key, 2), count)]


def bell_draw(rng, dims, width, limit, cuts=(), kind=jnp.bfloat16):
    values = jax.random.normal(rng, dims, jnp.float32) * width
    if len(cuts) > 0:
        values = level_of(rng, dims, cuts, -0.22, 0.18) * values
    return jnp.clip(values, min=-limit, max=limit).astype(kind)


def bell_draw_with(stream_key, dims, spread, most, split, heavy, held_as=jnp.bfloat16):
    values = spread * jax.random.normal(stream_key, dims, jnp.float32)
    if split:
        values = values * level_of(stream_key, dims, split, -0.22, 0.18)
    return jnp.clip(strengthened(values, jax.random.fold_in(stream_key, 3), *heavy), -most, most).astype(held_as)


def setup_inputs(seed: int = 0) -> dict:
    arg_keys = jax.random.split(jax.random.key(seed), 14)
    q_prompt = draw_q_prompt(jax.random.fold_in(arg_keys[13], 71), 0)
    k_prompt = draw_k_prompt(jax.random.fold_in(arg_keys[13], 71), 0)
    v_prompt = bell_draw(arg_keys[2], (PROMPT_ROWS, KV_HEADS * HEAD_DIM), 1.0, 6.0, ((0, 16), (1, 8)))
    do_prompt = bell_draw(arg_keys[3], (PROMPT_ROWS, HEADS * HEAD_DIM), 1.0, 6.0, ((0, 16), (1, 8)))
    q_resp = draw_q_resp(jax.random.fold_in(arg_keys[13], 71), 0)
    k_resp = draw_k_resp(jax.random.fold_in(arg_keys[13], 71), 0)
    v_resp = bell_draw(arg_keys[6], (RESP_ROWS, KV_HEADS * HEAD_DIM), 1.0, 6.0, ((0, 16), (1, 8)))
    do_resp = bell_draw(arg_keys[7], (RESP_ROWS, HEADS * HEAD_DIM), 1.0, 6.0, ((0, 16), (1, 8)))
    resp_lengths = jax.vmap(lambda own: uneven_parts(own, RESP_COUNT, RESP_DEV, MOST_LEN, 2))(jax.random.split(arg_keys[8], N_SEQ)).reshape((N_SEQ, RESP_COUNT)).astype(jnp.int32)
    resp_prompt = plant(jax.random.randint(arg_keys[9], (N_SEQ, RESP_COUNT), 0, PROMPTS), jax.random.fold_in(arg_keys[9], 1), 0, PROMPTS - 1).astype(jnp.int32)
    w_query = bell_draw_with(arg_keys[10], (D, HEADS * HEAD_DIM), HEAD_DIM ** -0.5, 0.75, ((1, 8),), (1, 0, 8, 2.0))
    w_key = bell_draw(arg_keys[11], (D, KV_HEADS * HEAD_DIM), HEAD_DIM ** -0.5, 0.5, ((1, 8),))
    w_value = bell_draw(arg_keys[12], (D, KV_HEADS * HEAD_DIM), HEAD_DIM ** -0.5, 0.5, ((1, 8),))
    return dict(q_prompt=q_prompt, k_prompt=k_prompt, v_prompt=v_prompt, do_prompt=do_prompt, q_resp=q_resp, k_resp=k_resp, v_resp=v_resp, do_resp=do_resp, resp_lengths=resp_lengths, resp_prompt=resp_prompt, w_query=w_query, w_key=w_key, w_value=w_value)


NEG = -1e+30

def rounded(x):
    return lax.optimization_barrier(x.astype(jnp.bfloat16)).astype(jnp.float32)

def einsum_hi(form, a, b):
    return jnp.einsum(form, a, b, precision=lax.Precision.HIGHEST)

def reference(q_prompt, k_prompt, v_prompt, do_prompt, q_resp, k_resp, v_resp, do_resp, resp_lengths, resp_prompt, w_query, w_key, w_value):
    group = HEADS // KV_HEADS
    scale = 1.0 / math.sqrt(HEAD_DIM)
    ends = jnp.cumsum(resp_lengths, axis=1)
    place = jnp.arange(RESP_DEV, dtype=jnp.int32)
    segment = lax.optimization_barrier(jnp.sum((place[None, :, None] >= ends[:, None, :]).astype(jnp.int32), axis=2))
    slots = jnp.arange(RESP_COUNT, dtype=jnp.int32)
    tok_prompt = lax.optimization_barrier(jnp.sum(jnp.where(segment[:, :, None] == slots[None, None, :], resp_prompt[:, None, :], 0), axis=2))
    key_index = jnp.arange(PROMPT_ROWS, dtype=jnp.int32)
    key_prompt = key_index // PROMPT_LEN
    mask_pp = (key_prompt[:, None] == key_prompt[None, :]) & (key_index[None, :] <= key_index[:, None])
    mask_rp = tok_prompt.reshape(-1)[:, None] == key_prompt[None, :]
    mask_rr = (segment[:, :, None] == segment[:, None, :]) & (place[None, None, :] <= place[None, :, None])

    def heads_first(x, rows):
        return x.astype(jnp.float32).reshape(rows, KV_HEADS, group, HEAD_DIM).transpose(1, 2, 0, 3)

    def kv_first(x, rows):
        return x.astype(jnp.float32).reshape(rows, KV_HEADS, HEAD_DIM).transpose(1, 0, 2)

    def per_head(inputs):
        qp, kp, vp, dop, qr, kr, vr, dor = inputs
        qr4 = qr.reshape(group, N_SEQ, RESP_DEV, HEAD_DIM)
        dor4 = dor.reshape(group, N_SEQ, RESP_DEV, HEAD_DIM)
        kr3 = kr.reshape(N_SEQ, RESP_DEV, HEAD_DIM)
        vr3 = vr.reshape(N_SEQ, RESP_DEV, HEAD_DIM)
        s_pp = einsum_hi('gqd,kd->gqk', qp, kp) * scale
        dp_pp = einsum_hi('gqd,kd->gqk', dop, vp)
        s_rp = einsum_hi('gqd,kd->gqk', qr, kp) * scale
        dp_rp = einsum_hi('gqd,kd->gqk', dor, vp)
        s_rr = einsum_hi('gnqd,nkd->gnqk', qr4, kr3) * scale
        dp_rr = einsum_hi('gnqd,nkd->gnqk', dor4, vr3)
        top_p = lax.optimization_barrier(jnp.max(jnp.where(mask_pp, s_pp, NEG), axis=-1))
        top_r = jnp.maximum(lax.optimization_barrier(jnp.max(jnp.where(mask_rp, s_rp, NEG), axis=-1)), lax.optimization_barrier(jnp.max(jnp.where(mask_rr, s_rr, NEG), axis=-1)).reshape(group, RESP_ROWS))
        top_rr = top_r.reshape(group, N_SEQ, RESP_DEV)
        e_pp = jnp.where(mask_pp, jnp.exp(s_pp - top_p[..., None]), 0.0)
        e_rp = jnp.where(mask_rp, jnp.exp(s_rp - top_r[..., None]), 0.0)
        e_rr = jnp.where(mask_rr, jnp.exp(s_rr - top_rr[..., None]), 0.0)
        total_p = lax.optimization_barrier(jnp.sum(e_pp, axis=-1))
        total_r = lax.optimization_barrier(jnp.sum(e_rp, axis=-1)) + lax.optimization_barrier(jnp.sum(e_rr, axis=-1)).reshape(group, RESP_ROWS)
        mean_p = lax.optimization_barrier(jnp.sum(e_pp * dp_pp, axis=-1)) / total_p
        mean_r = (lax.optimization_barrier(jnp.sum(e_rp * dp_rp, axis=-1)) + lax.optimization_barrier(jnp.sum(e_rr * dp_rr, axis=-1)).reshape(group, RESP_ROWS)) / total_r
        total_rr = total_r.reshape(group, N_SEQ, RESP_DEV)
        mean_rr = mean_r.reshape(group, N_SEQ, RESP_DEV)
        prob_pp = e_pp / total_p[..., None]
        prob_rp = e_rp / total_r[..., None]
        prob_rr = e_rr / total_rr[..., None]
        ds_pp = rounded(prob_pp * (dp_pp - mean_p[..., None]) * scale)
        ds_rp = rounded(prob_rp * (dp_rp - mean_r[..., None]) * scale)
        ds_rr = rounded(prob_rr * (dp_rr - mean_rr[..., None]) * scale)
        pb_pp = rounded(prob_pp)
        pb_rp = rounded(prob_rp)
        pb_rr = rounded(prob_rr)
        dq_p = einsum_hi('gqk,kd->gqd', ds_pp, kp)
        dq_r = einsum_hi('gqk,kd->gqd', ds_rp, kp) + einsum_hi('gnqk,nkd->gnqd', ds_rr, kr3).reshape(group, RESP_ROWS, HEAD_DIM)
        dk_p = einsum_hi('gqk,gqd->kd', ds_pp, qp) + einsum_hi('gqk,gqd->kd', ds_rp, qr)
        dv_p = einsum_hi('gqk,gqd->kd', pb_pp, dop) + einsum_hi('gqk,gqd->kd', pb_rp, dor)
        dk_r = einsum_hi('gnqk,gnqd->nkd', ds_rr, qr4).reshape(RESP_ROWS, HEAD_DIM)
        dv_r = einsum_hi('gnqk,gnqd->nkd', pb_rr, dor4).reshape(RESP_ROWS, HEAD_DIM)
        return (dq_p, dq_r, dk_p, dv_p, dk_r, dv_r)
    stacked = (heads_first(q_prompt, PROMPT_ROWS), kv_first(k_prompt, PROMPT_ROWS), kv_first(v_prompt, PROMPT_ROWS), heads_first(do_prompt, PROMPT_ROWS), heads_first(q_resp, RESP_ROWS), kv_first(k_resp, RESP_ROWS), kv_first(v_resp, RESP_ROWS), heads_first(do_resp, RESP_ROWS))
    dq_p, dq_r, dk_p, dv_p, dk_r, dv_r = lax.map(per_head, stacked)

    def query_back(x, rows):
        return x.transpose(2, 0, 1, 3).reshape(rows, HEADS * HEAD_DIM).astype(jnp.bfloat16)

    def kv_back(x, rows):
        return x.transpose(1, 0, 2).reshape(rows, KV_HEADS * HEAD_DIM).astype(jnp.bfloat16)

    def input_grad(dq, dk, dv):
        qwide = HEADS * HEAD_DIM // N_HEAD
        kwide = KV_HEADS * HEAD_DIM // N_HEAD
        total = jnp.zeros((dq.shape[0], D), jnp.float32)
        for index in range(N_HEAD):
            qs = slice(index * qwide, (index + 1) * qwide)
            ks = slice(index * kwide, (index + 1) * kwide)
            term = jnp.dot(dq[:, qs], w_query[:, qs].T, preferred_element_type=jnp.float32)
            term = term + jnp.dot(dk[:, ks], w_key[:, ks].T, preferred_element_type=jnp.float32)
            term = term + jnp.dot(dv[:, ks], w_value[:, ks].T, preferred_element_type=jnp.float32)
            total = total + rounded(term)
        return total.astype(jnp.bfloat16)
    dx_prompt = input_grad(query_back(dq_p, PROMPT_ROWS), kv_back(dk_p, PROMPT_ROWS), kv_back(dv_p, PROMPT_ROWS))
    dx_resp = input_grad(query_back(dq_r, RESP_ROWS), kv_back(dk_r, RESP_ROWS), kv_back(dv_r, RESP_ROWS))
    return (dx_prompt, dx_resp)
```

```python
import functools
import math

import jax
import jax.numpy as jnp
from jax import lax
from jax.experimental import pallas as pl
from jax.experimental.pallas import tpu as pltpu
from jax.sharding import PartitionSpec as P

MESH = pl.DeviceIdType.MESH
VMEM = pltpu.VMEM
BF16 = jnp.bfloat16
F32 = jnp.float32
HD = 128
GROUP = 8
TOK = 128
NEG = -1e30
SCALE = 1.0 / math.sqrt(HD)
EXP2 = SCALE * math.log2(math.e)
D = 5120
COLS = 640
WIDE = 1280
NT = (((1,), (1,)), ((), ()))
NN = (((1,), (0,)), ((), ()))


def dot(a, b, dims):
    return lax.dot_general(a, b, dims, preferred_element_type=F32)


def remote(src, dst, send, recv, seq, head):
    return pltpu.make_async_remote_copy(
        src_ref=src, dst_ref=dst, send_sem=send, recv_sem=recv,
        device_id=(seq, head), device_id_type=MESH,
    )


def seq_place():
    n = lax.axis_index("seq")
    return n // 4, lax.rem(n // 2, 2), lax.rem(n, 2)


def seq_peer(dy, dx):
    y, x, c = seq_place()
    return lax.rem(y + dy + 4, 4) * 4 + lax.rem(x + dx, 2) * 2 + c


def seq_sibling():
    n = lax.axis_index("seq")
    return n + 1 - 2 * lax.rem(n, 2)


SEQ_STEPS = [(0, 1), (1, 0), (3, 0), (1, 1), (3, 1), (2, 0), (2, 1)]


def head_peers():
    h = lax.axis_index("head")
    x, z = h // 4, lax.rem(h, 4)
    base = x * 4
    z1 = base + z + 1 - 2 * lax.rem(z, 2)
    z3 = base + 3 - z
    flip = (1 - x) * 4 + z
    return z1, z3, flip


def gather_copies(kv, send, recv, fsend, frecv):
    n, head = lax.axis_index("seq"), lax.axis_index("head")
    sib = seq_sibling()
    firsts = [remote(kv.at[n], kv.at[n], fsend.at[0], frecv.at[0], sib, head)]
    for j, (dy, dx) in enumerate(SEQ_STEPS):
        firsts.append(
            remote(kv.at[n], kv.at[n], send.at[j], recv.at[j], seq_peer(dy, dx), head)
        )
    return firsts


def gather_start(kv, send, recv, fsend, frecv):
    for copy in gather_copies(kv, send, recv, fsend, frecv):
        copy.start()


def gather_finish(kv, send, recv, fsend, frecv):
    head = lax.axis_index("head")
    sib = seq_sibling()
    firsts = gather_copies(kv, send, recv, fsend, frecv)
    forwards = []
    for j, (dy, dx) in enumerate(SEQ_STEPS):
        src = seq_peer(-dy, dx)
        firsts[j + 1].wait_recv()
        forward = remote(kv.at[src], kv.at[src], fsend.at[j + 1], frecv.at[j + 1], sib, head)
        forward.start()
        forwards.append(forward)
    for copy in [firsts[0]] + forwards:
        copy.wait_recv()
    for copy in firsts + forwards:
        copy.wait_send()


def gather_kernel(k_ref, v_ref, kv, send, recv, fsend, frecv):
    n, head = lax.axis_index("seq"), lax.axis_index("head")
    kv[n, 0] = k_ref[...]
    kv[n, 1] = v_ref[...]
    barrier = pltpu.get_barrier_semaphore()
    peers = [seq_sibling()] + [seq_peer(dy, dx) for dy, dx in SEQ_STEPS]
    for peer in peers:
        pl.semaphore_signal(barrier, inc=1, device_id=(peer, head), device_id_type=MESH)
    pl.semaphore_wait(barrier, len(peers))
    gather_start(kv, send, recv, fsend, frecv)
    gather_finish(kv, send, recv, fsend, frecv)


def gather(k, v):
    return pl.pallas_call(
        gather_kernel,
        out_shape=jax.ShapeDtypeStruct((16, 2, TOK, HD), BF16),
        in_specs=[pl.BlockSpec(memory_space=VMEM)] * 2,
        out_specs=pl.BlockSpec(memory_space=VMEM),
        scratch_shapes=[
            pltpu.SemaphoreType.DMA((7,)),
            pltpu.SemaphoreType.DMA((7,)),
            pltpu.SemaphoreType.DMA((8,)),
            pltpu.SemaphoreType.DMA((8,)),
        ],
        compiler_params=pltpu.CompilerParams(
            collective_id=0, has_side_effects=True, vmem_limit_bytes=32 << 20
        ),
        name="gather_kv",
    )(k, v)


def segment_of(place, lens_ref):
    end = jnp.int32(0)
    seg = jnp.zeros(place.shape, jnp.int32)
    for c in range(4):
        end = end + lens_ref[0, c]
        seg = seg + (place >= end).astype(jnp.int32)
    return seg


def prompt_of(seg, prompt_ref):
    out = jnp.zeros(seg.shape, jnp.int32)
    for c in range(4):
        out = jnp.where(seg == c, prompt_ref[0, c], out)
    return out


def load_keys(kv, k_r, v_r, kke, vve, kket):
    for r in range(8):
        rows = pl.ds(r * TOK, TOK)
        kke[rows, :HD] = kv[r, 0]
        kke[rows, HD:] = kv[8 + r, 0]
        vve[rows, :HD] = kv[r, 1]
        vve[rows, HD:] = kv[8 + r, 1]
    local = pl.ds(1024, 256)
    kke[local, :HD] = k_r[...]
    kke[local, HD:] = k_r[...]
    vve[local, :HD] = v_r[...]
    vve[local, HD:] = v_r[...]
    for r in range(10):
        rows = pl.ds(r * TOK, TOK)
        kket[:, rows] = kke[rows, :].T


def load_rows(q, do, col_prompt, qext, doext):
    first = col_prompt == 0
    zero = jnp.zeros((TOK, HD), BF16)
    first = jnp.broadcast_to(first, (TOK, HD))
    for h in range(GROUP):
        lanes = pl.ds(h * HD, HD)
        rows = pl.ds(h * TOK, TOK)
        qv, dov = q[:, lanes], do[:, lanes]
        qext[rows, :HD] = jnp.where(first, qv, zero)
        qext[rows, HD:] = jnp.where(first, zero, qv)
        doext[rows, :HD] = jnp.where(first, dov, zero)
        doext[rows, HD:] = jnp.where(first, zero, dov)


def fold(x, op):
    return op(x.reshape(TOK // 8, 8, x.shape[1]), axis=0)


def head_pair(hp, tiles, bias_of, qext, doext, kke, vve, s_ref, dp_ref, et, dst):
    rows = pl.ds(pl.multiple_of(hp * 256, 256), 256)
    qe, doe = qext[rows, :], doext[rows, :]
    top = jnp.full((8, 256), NEG, F32)
    for t in range(tiles):
        keys = pl.ds(t * TOK, TOK)
        s = dot(kke[keys, :], qe, NT)
        s = bias_of(t, s)
        s_ref[keys, :] = s
        top = jnp.maximum(top, fold(s, jnp.max))
        dp_ref[keys, :] = dot(vve[keys, :], doe, NT)
    top = jnp.max(top, axis=0, keepdims=True)
    norm = jnp.zeros((8, 256), F32)
    weighted = jnp.zeros((8, 256), F32)
    for t in range(tiles):
        keys = pl.ds(t * TOK, TOK)
        e = jnp.exp2((s_ref[keys, :] - top) * EXP2)
        s_ref[keys, :] = e
        norm = norm + fold(e, jnp.sum)
        weighted = weighted + fold(e * dp_ref[keys, :], jnp.sum)
    inv = 1.0 / jnp.sum(norm, axis=0, keepdims=True)
    mean = jnp.sum(weighted, axis=0, keepdims=True) * inv
    for t in range(tiles):
        keys = pl.ds(t * TOK, TOK)
        p = s_ref[keys, :] * inv
        et[keys, rows] = p.astype(BF16)
        dst[keys, rows] = (p * (dp_ref[keys, :] - mean)).astype(BF16)


def chunk_products(tiles, first, qext, doext, kket, et, dst, dkk, dvv):
    for t in range(tiles):
        keys = pl.ds(t * TOK, TOK)
        dv = dot(et[keys, :], doext[...], NN)
        dk = dot(dst[keys, :], qext[...], NN)
        if first:
            dvv[keys, :] = dv
            dkk[keys, :] = dk
        else:
            dvv[keys, :] += dv
            dkk[keys, :] += dk


def chunk_dq(tiles, row_prompt, kket, dst, dq_ref, rows_out):
    keys = pl.ds(0, tiles * TOK)
    first = row_prompt == 0
    for hp in range(4):
        rows = pl.ds(hp * 256, 256)
        both = dot(kket[:, keys], dst[keys, rows], NN)
        for k in range(2):
            lanes = slice(k * TOK, (k + 1) * TOK)
            part = jnp.where(first, both[:HD, lanes], both[HD:, lanes]) * SCALE
            h = hp * 2 + k
            dq_ref[rows_out, h * HD : (h + 1) * HD] = part.T.astype(BF16)


def attention_kernel(
    lens_ref, prompt_ref, kv, q_p, do_p, q_r, do_r, k_r, v_r,
    d_r, dq_p, grads,
    kke, vve, kket, qext, doext, s_ref, dp_ref, et, dst, dkk, dvv, bias,
):
    n = lax.axis_index("seq")
    load_keys(kv, k_r, v_r, kke, vve, kket)

    for number, half in enumerate((1, 0)):
        tiles = 8 + half + 1
        count = (half + 1) * TOK
        base = half * TOK
        col = base + lax.broadcasted_iota(jnp.int32, (TOK, 1), 0)
        col_prompt = prompt_of(segment_of(col, lens_ref), prompt_ref)
        row = base + lax.rem(lax.broadcasted_iota(jnp.int32, (1, 256), 1), TOK)
        row_seg = segment_of(row, lens_ref)
        row_prompt = prompt_of(row_seg[:, :TOK], prompt_ref)
        key = lax.broadcasted_iota(jnp.int32, (count, 1), 0)
        key_seg = segment_of(key, lens_ref)
        seen = (key_seg == row_seg) & (key <= row)
        bias[:count, :] = jnp.where(seen, 0.0, NEG)
        span = slice(base, base + TOK)
        load_rows(q_r.at[span], do_r.at[span], col_prompt, qext, doext)

        def local_bias(t, s):
            if t < 8:
                return s
            return s + bias[(t - 8) * TOK : (t - 7) * TOK, :]

        def visit(hp, c):
            head_pair(
                hp, tiles, local_bias, qext, doext, kke, vve, s_ref, dp_ref, et, dst
            )
            return c

        lax.fori_loop(0, 4, visit, 0)
        if number == 0:
            chunk_products(tiles, True, qext, doext, kket, et, dst, dkk, dvv)
        else:
            chunk_products(tiles, False, qext, doext, kket, et, dst, dkk, dvv)
        chunk_dq(tiles, row_prompt, kket, dst, d_r, span)

    place = lax.rem(n, 8) * TOK
    diff = (
        place
        + lax.rem(lax.broadcasted_iota(jnp.int32, (TOK, 256), 1), TOK)
        - lax.broadcasted_iota(jnp.int32, (TOK, 256), 0)
    )
    mine = n // 8
    load_rows(q_p, do_p, jnp.full((TOK, 1), mine, jnp.int32), qext, doext)

    def causal(t, s):
        return jnp.where(diff >= t * TOK, s, NEG)

    def visit(hp, c):
        head_pair(hp, 8, causal, qext, doext, kke, vve, s_ref, dp_ref, et, dst)
        return c

    lax.fori_loop(0, 4, visit, 0)
    chunk_products(8, False, qext, doext, kket, et, dst, dkk, dvv)
    chunk_dq(8, jnp.full((1, TOK), mine, jnp.int32), kket, dst, dq_p, slice(0, TOK))

    local = slice(1024, WIDE)
    d_r[:, 1024:1152] = ((dkk[local, :HD] + dkk[local, HD:]) * SCALE).astype(BF16)
    d_r[:, 1152:] = (dvv[local, :HD] + dvv[local, HD:]).astype(BF16)
    for r in range(8):
        keys = slice(r * TOK, (r + 1) * TOK)
        for p in range(2):
            lanes = slice(p * HD, (p + 1) * HD)
            grads[r, p, :, :HD] = (dkk[keys, lanes] * SCALE).astype(BF16)
            grads[r, p, :, HD:] = dvv[keys, lanes].astype(BF16)


def attention(lens, prompts, kv, q_p, do_p, q_r, do_r, k_r, v_r):
    whole = pl.BlockSpec(memory_space=VMEM)
    scalars = pl.BlockSpec(memory_space=pltpu.SMEM)
    return pl.pallas_call(
        attention_kernel,
        out_shape=(
            jax.ShapeDtypeStruct((256, WIDE), BF16),
            jax.ShapeDtypeStruct((TOK, 1024), BF16),
            jax.ShapeDtypeStruct((8, 2, TOK, 256), BF16),
        ),
        in_specs=[scalars] * 2 + [whole] * 7,
        out_specs=(whole,) * 3,
        scratch_shapes=[
            VMEM((WIDE, 256), BF16),
            VMEM((WIDE, 256), BF16),
            VMEM((256, WIDE), BF16),
            VMEM((1024, 256), BF16),
            VMEM((1024, 256), BF16),
            VMEM((WIDE, 256), F32),
            VMEM((WIDE, 256), F32),
            VMEM((WIDE, 1024), BF16),
            VMEM((WIDE, 1024), BF16),
            VMEM((WIDE, 256), F32),
            VMEM((WIDE, 256), F32),
            VMEM((256, 256), F32),
        ],
        compiler_params=pltpu.CompilerParams(vmem_limit_bytes=48 << 20),
        name="attention",
    )(lens, prompts, kv, q_p, do_p, q_r, do_r, k_r, v_r)


SIDES = (
    dict(give=(1, 3), keep=(0, 3), last=1),
    dict(give=(2, 4), keep=(1, 0), last=0),
)


def owner_of(offset, side):
    h = lax.axis_index("head")
    x, z = h // 4, lax.rem(h, 4)
    if offset == 0:
        oz = z
    elif offset == 1:
        oz = z + 1 - 2 * lax.rem(z, 2)
    elif offset == 2:
        oz = lax.rem(z + 2, 4)
    else:
        oz = 3 - z
    ox = x if side == 0 else 1 - x
    return ox * 4 + oz


WEIGHT_ORDER = (2, 1, 3, 0)


def weight_copies(offsets, w_q, w_k, w_v, w, sem):
    for offset in offsets:
        for side in range(2):
            rows = pl.ds(pl.multiple_of(owner_of(offset, side) * COLS, COLS), COLS)
            into = pl.ds(side * COLS, COLS)
            yield from [
                pltpu.make_async_copy(w_q.at[rows], w.at[offset, into, pl.ds(0, 1024)], sem.at[offset, side, 0]),
                pltpu.make_async_copy(w_k.at[rows], w.at[offset, into, pl.ds(1024, HD)], sem.at[offset, side, 1]),
                pltpu.make_async_copy(w_v.at[rows], w.at[offset, into, pl.ds(1152, HD)], sem.at[offset, side, 2]),
            ]


class HeadSum:
    def __init__(self, chunk, terms, r1, s2, r2, s3, r3, sems):
        self.chunk = chunk
        self.terms, self.r1, self.s2, self.r2, self.s3, self.r3 = (
            terms.at[chunk], r1.at[chunk], s2.at[chunk], r2.at[chunk], s3.at[chunk], r3.at[chunk]
        )
        self.sems = sems
        self.seq = lax.axis_index("seq")
        self.z1, self.z3, self.flip = head_peers()

    def copy(self, half, step):
        send, recv = (self.sems.at[k, self.chunk, half, step] for k in range(2))
        near, far = (self.z1, self.z3) if half == 0 else (self.z3, self.z1)
        if step == 0:
            low, high = SIDES[half]["give"]
            src = self.terms.at[pl.ds(low, high - low), :, pl.ds(half * 64, 64), :]
            return remote(src, self.r1.at[half], send, recv, self.seq, near)
        if step == 1:
            return remote(self.s2.at[half], self.r2.at[half], send, recv, self.seq, self.flip)
        return remote(self.s3.at[half], self.r3.at[half], send, recv, self.seq, far)

    def first(self, half):
        self.copy(half, 0).start()

    def second(self, half):
        self.copy(half, 0).wait_recv()
        rows = slice(half * 64, half * 64 + 64)
        for k, offset in enumerate(SIDES[half]["keep"]):
            total = self.terms[offset, 1, rows, :].astype(F32) + self.r1[half, k, 1].astype(F32)
            self.s2[half, k] = total.astype(BF16)
        self.copy(half, 1).start()

    def kept(self, half, k):
        rows = slice(half * 64, half * 64 + 64)
        offset = SIDES[half]["keep"][k]
        return (
            self.terms[offset, 0, rows, :].astype(F32)
            + self.r1[half, k, 0].astype(F32)
            + self.r2[half, k].astype(F32)
        )

    def third(self, half):
        self.copy(half, 1).wait_recv()
        self.s3[half] = self.kept(half, SIDES[half]["last"]).astype(BF16)
        self.copy(half, 2).start()

    def final(self, half, out, base):
        total = self.kept(half, 1 - SIDES[half]["last"])
        self.copy(half, 2).wait_recv()
        out[base + half * 64 : base + half * 64 + 64, :] = (
            total + self.r3[half].astype(F32)
        ).astype(BF16)

    def drain(self):
        for half in range(2):
            for step in range(3):
                self.copy(half, step).wait_send()


def project(d, w, terms, chunk, wait_weights):
    rows = d[...]
    for offset in WEIGHT_ORDER:
        wait_weights(offset)
        for part in range(5):
            block = dot(rows, w[offset, part * 256 : (part + 1) * 256, :], NT).astype(BF16)
            for piece in range(2):
                col = part * 256 + piece * 128
                side, lane = divmod(col, COLS)
                terms[chunk, offset, side, :, lane : lane + 128] = block[:, piece * 128 : piece * 128 + 128]


def grads_sibling(grads, rc, gsem):
    c = lax.rem(lax.axis_index("seq"), 2)
    return remote(
        grads.at[:, 1 - c], rc, gsem.at[0, 7], gsem.at[1, 7], seq_sibling(), lax.axis_index("head")
    )


def grads_copies(gs, rg, gsem):
    y, x, c = seq_place()
    copies = []
    for j, (dy, dx) in enumerate(SEQ_STEPS):
        oy = lax.rem(y + dy, 4)
        ox = lax.rem(x + dx, 2)
        block = lax.rem(oy, 2) * 2 + ox
        copies.append(
            remote(
                gs.at[block, oy // 2], rg.at[j], gsem.at[0, j], gsem.at[1, j],
                seq_peer(dy, dx), lax.axis_index("head"),
            )
        )
    return copies


def grads_second(grads, rc, gs, rg, gsem):
    c = lax.rem(lax.axis_index("seq"), 2)
    grads_sibling(grads, rc, gsem).wait_recv()
    for b in range(4):
        for p in range(2):
            gs[b, p] = (grads[b, c, p].astype(F32) + rc[b, p].astype(F32)).astype(BF16)
    for copy in grads_copies(gs, rg, gsem):
        copy.start()


def grads_finish(gs, rg, gsem, d_p):
    y, x, c = seq_place()
    total = gs[lax.rem(y, 2) * 2 + x, y // 2].astype(F32)
    for j, copy in enumerate(grads_copies(gs, rg, gsem)):
        copy.wait_recv()
        total = total + rg[j].astype(F32)
    d_p[:, 1024:] = total.astype(BF16)


def project_kernel(
    d_r, dq_p, grads, w_q, w_k, w_v,
    out_p, out_r,
    w, d_p, terms, r1, s2, r2, s3, r3, rc, gs, rg, wsem, hsem, gsem,
):
    seq, head = lax.axis_index("seq"), lax.axis_index("head")
    for copy in weight_copies(WEIGHT_ORDER, w_q, w_k, w_v, w, wsem):
        copy.start()
    barrier = pltpu.get_barrier_semaphore()
    seqs = [seq_sibling()] + [seq_peer(dy, dx) for dy, dx in SEQ_STEPS]
    heads = list(head_peers())
    for peer in seqs:
        pl.semaphore_signal(barrier, inc=1, device_id=(peer, head), device_id_type=MESH)
    for peer in heads:
        pl.semaphore_signal(barrier, inc=1, device_id=(seq, peer), device_id_type=MESH)
    pl.semaphore_wait(barrier, len(seqs) + len(heads))

    grads_sibling(grads, rc, gsem).start()
    d_p[:, :1024] = dq_p[...]

    def wait_weights(offset):
        for copy in weight_copies((offset,), w_q, w_k, w_v, w, wsem):
            copy.wait()

    sums = [HeadSum(c, terms, r1, s2, r2, s3, r3, hsem) for c in range(3)]
    project(d_r.at[0:TOK], w, terms, 0, wait_weights)
    for half in range(2):
        sums[0].first(half)
    grads_second(grads, rc, gs, rg, gsem)
    project(d_r.at[TOK:256], w, terms, 1, lambda offset: None)
    for half in range(2):
        sums[1].first(half)
    grads_finish(gs, rg, gsem, d_p)
    project(d_p, w, terms, 2, lambda offset: None)
    for half in range(2):
        sums[2].first(half)
    for c in range(3):
        for half in range(2):
            sums[c].second(half)
    for c in range(3):
        for half in range(2):
            sums[c].third(half)
    for c in range(3):
        out, base = (out_p, 0) if c == 2 else (out_r, c * TOK)
        for half in range(2):
            sums[c].final(half, out, base)
    grads_sibling(grads, rc, gsem).wait_send()
    for copy in grads_copies(gs, rg, gsem):
        copy.wait_send()
    for c in range(3):
        sums[c].drain()


def projection(d_r, dq_p, grads, w_q, w_k, w_v):
    whole = pl.BlockSpec(memory_space=VMEM)
    hbm = pl.BlockSpec(memory_space=pl.ANY)
    return pl.pallas_call(
        project_kernel,
        out_shape=(
            jax.ShapeDtypeStruct((TOK, COLS), BF16),
            jax.ShapeDtypeStruct((256, COLS), BF16),
        ),
        in_specs=[whole] * 3 + [hbm] * 3,
        out_specs=(whole,) * 2,
        scratch_shapes=[
            VMEM((4, WIDE, WIDE), BF16),
            VMEM((TOK, WIDE), BF16),
            VMEM((3, 4, 2, TOK, COLS), BF16),
            VMEM((3, 2, 2, 2, 64, COLS), BF16),
            VMEM((3, 2, 2, 64, COLS), BF16),
            VMEM((3, 2, 2, 64, COLS), BF16),
            VMEM((3, 2, 64, COLS), BF16),
            VMEM((3, 2, 64, COLS), BF16),
            VMEM((4, 2, TOK, 256), BF16),
            VMEM((4, 2, TOK, 256), BF16),
            VMEM((7, TOK, 256), BF16),
            pltpu.SemaphoreType.DMA((4, 2, 3)),
            pltpu.SemaphoreType.DMA((2, 3, 2, 3)),
            pltpu.SemaphoreType.DMA((2, 8)),
        ],
        compiler_params=pltpu.CompilerParams(
            collective_id=1, has_side_effects=True, vmem_limit_bytes=56 << 20
        ),
        name="project_sum",
    )(d_r, dq_p, grads, w_q, w_k, w_v)


def shards(
    q_prompt, k_prompt, v_prompt, do_prompt, q_resp, k_resp, v_resp, do_resp,
    resp_lengths, resp_prompt, w_query, w_key, w_value,
):
    kv = gather(k_prompt, v_prompt)
    d_r, dq_p, grads = attention(
        resp_lengths, resp_prompt, kv, q_prompt, do_prompt, q_resp, do_resp, k_resp, v_resp
    )
    grads = grads.reshape(4, 2, 2, TOK, 256)
    return projection(d_r, dq_p, grads, w_query, w_key, w_value)


def solution(mesh):
    return jax.shard_map(
        shards,
        mesh=mesh,
        in_specs=(P("seq", "head"),) * 8 + (P("seq", None),) * 2 + (P(None, "head"),) * 3,
        out_specs=(P("seq", "head"), P("seq", "head")),
        check_vma=False,
    )
```

```python
import functools
import math

import jax
import jax.numpy as jnp
from jax import lax
from jax.experimental import pallas as pl
from jax.experimental.pallas import tpu as pltpu
from jax.sharding import PartitionSpec as P

MESH = pl.DeviceIdType.MESH
VMEM = pltpu.VMEM
BF16 = jnp.bfloat16
F32 = jnp.float32
HD = 128
GROUP = 8
TOK = 128
NEG = -1e30
SCALE = 1.0 / math.sqrt(HD)
EXP2 = SCALE * math.log2(math.e)
D = 5120
COLS = 640
WIDE = 1280
NT = (((1,), (1,)), ((), ()))
NN = (((1,), (0,)), ((), ()))


def dot(a, b, dims):
    return lax.dot_general(a, b, dims, preferred_element_type=F32)


def remote(src, dst, send, recv, seq, head):
    return pltpu.make_async_remote_copy(
        src_ref=src, dst_ref=dst, send_sem=send, recv_sem=recv,
        device_id=(seq, head), device_id_type=MESH,
    )


def seq_place():
    n = lax.axis_index("seq")
    return n // 4, lax.rem(n // 2, 2), lax.rem(n, 2)


def seq_peer(dy, dx):
    y, x, c = seq_place()
    return lax.rem(y + dy + 4, 4) * 4 + lax.rem(x + dx, 2) * 2 + c


def seq_sibling():
    n = lax.axis_index("seq")
    return n + 1 - 2 * lax.rem(n, 2)


SEQ_STEPS = [(0, 1), (1, 0), (3, 0), (1, 1), (3, 1), (2, 0), (2, 1)]


def head_peers():
    h = lax.axis_index("head")
    x, z = h // 4, lax.rem(h, 4)
    base = x * 4
    z1 = base + z + 1 - 2 * lax.rem(z, 2)
    z3 = base + 3 - z
    flip = (1 - x) * 4 + z
    return z1, z3, flip


def gather_copies(kv, send, recv, fsend, frecv):
    n, head = lax.axis_index("seq"), lax.axis_index("head")
    sib = seq_sibling()
    firsts = [remote(kv.at[n], kv.at[n], fsend.at[0], frecv.at[0], sib, head)]
    for j, (dy, dx) in enumerate(SEQ_STEPS):
        firsts.append(
            remote(kv.at[n], kv.at[n], send.at[j], recv.at[j], seq_peer(dy, dx), head)
        )
    return firsts


def gather_start(kv, send, recv, fsend, frecv):
    for copy in gather_copies(kv, send, recv, fsend, frecv):
        copy.start()


def gather_finish(kv, send, recv, fsend, frecv):
    head = lax.axis_index("head")
    sib = seq_sibling()
    firsts = gather_copies(kv, send, recv, fsend, frecv)
    forwards = []
    for j, (dy, dx) in enumerate(SEQ_STEPS):
        src = seq_peer(-dy, dx)
        firsts[j + 1].wait_recv()
        forward = remote(kv.at[src], kv.at[src], fsend.at[j + 1], frecv.at[j + 1], sib, head)
        forward.start()
        forwards.append(forward)
    for copy in [firsts[0]] + forwards:
        copy.wait_recv()
    for copy in firsts + forwards:
        copy.wait_send()


def segment_of(place, lens_ref):
    end = jnp.int32(0)
    seg = jnp.zeros(place.shape, jnp.int32)
    for c in range(4):
        end = end + lens_ref[0, c]
        seg = seg + (place >= end).astype(jnp.int32)
    return seg


def prompt_of(seg, prompt_ref):
    out = jnp.zeros(seg.shape, jnp.int32)
    for c in range(4):
        out = jnp.where(seg == c, prompt_ref[0, c], out)
    return out


def load_keys(kv, k_r, v_r, kke, vve, kket):
    for r in range(8):
        rows = pl.ds(r * TOK, TOK)
        kke[rows, :HD] = kv[r, 0]
        kke[rows, HD:] = kv[8 + r, 0]
        vve[rows, :HD] = kv[r, 1]
        vve[rows, HD:] = kv[8 + r, 1]
    local = pl.ds(1024, 256)
    kke[local, :HD] = k_r[...]
    kke[local, HD:] = k_r[...]
    vve[local, :HD] = v_r[...]
    vve[local, HD:] = v_r[...]
    for r in range(10):
        rows = pl.ds(r * TOK, TOK)
        kket[:, rows] = kke[rows, :].T


def load_rows(q, do, col_prompt, qext, doext):
    first = col_prompt == 0
    zero = jnp.zeros((TOK, HD), BF16)
    first = jnp.broadcast_to(first, (TOK, HD))
    for h in range(GROUP):
        lanes = pl.ds(h * HD, HD)
        rows = pl.ds(h * TOK, TOK)
        qv, dov = q[:, lanes], do[:, lanes]
        qext[rows, :HD] = jnp.where(first, qv, zero)
        qext[rows, HD:] = jnp.where(first, zero, qv)
        doext[rows, :HD] = jnp.where(first, dov, zero)
        doext[rows, HD:] = jnp.where(first, zero, dov)


def fold(x, op):
    return op(x.reshape(TOK // 8, 8, x.shape[1]), axis=0)


def head_pair(hp, tiles, bias_of, qext, doext, kke, vve, s_ref, dp_ref, et, dst):
    rows = pl.ds(pl.multiple_of(hp * 256, 256), 256)
    qe, doe = qext[rows, :], doext[rows, :]
    top = jnp.full((8, 256), NEG, F32)
    for t in range(tiles):
        keys = pl.ds(t * TOK, TOK)
        s = dot(kke[keys, :], qe, NT)
        s = bias_of(t, s)
        s_ref[keys, :] = s
        top = jnp.maximum(top, fold(s, jnp.max))
        dp_ref[keys, :] = dot(vve[keys, :], doe, NT)
    top = jnp.max(top, axis=0, keepdims=True)
    norm = jnp.zeros((8, 256), F32)
    weighted = jnp.zeros((8, 256), F32)
    for t in range(tiles):
        keys = pl.ds(t * TOK, TOK)
        e = jnp.exp2((s_ref[keys, :] - top) * EXP2)
        s_ref[keys, :] = e
        norm = norm + fold(e, jnp.sum)
        weighted = weighted + fold(e * dp_ref[keys, :], jnp.sum)
    inv = 1.0 / jnp.sum(norm, axis=0, keepdims=True)
    mean = jnp.sum(weighted, axis=0, keepdims=True) * inv
    for t in range(tiles):
        keys = pl.ds(t * TOK, TOK)
        p = s_ref[keys, :] * inv
        et[keys, rows] = p.astype(BF16)
        dst[keys, rows] = (p * (dp_ref[keys, :] - mean)).astype(BF16)


def chunk_products(tiles, first, qext, doext, kket, et, dst, dkk, dvv):
    for t in range(tiles):
        keys = pl.ds(t * TOK, TOK)
        dv = dot(et[keys, :], doext[...], NN)
        dk = dot(dst[keys, :], qext[...], NN)
        if first:
            dvv[keys, :] = dv
            dkk[keys, :] = dk
        else:
            dvv[keys, :] += dv
            dkk[keys, :] += dk


def chunk_dq(tiles, row_prompt, kket, dst, dq_ref, rows_out):
    keys = pl.ds(0, tiles * TOK)
    first = row_prompt == 0
    for hp in range(4):
        rows = pl.ds(hp * 256, 256)
        both = dot(kket[:, keys], dst[keys, rows], NN)
        for k in range(2):
            lanes = slice(k * TOK, (k + 1) * TOK)
            part = jnp.where(first, both[:HD, lanes], both[HD:, lanes]) * SCALE
            h = hp * 2 + k
            dq_ref[rows_out, h * HD : (h + 1) * HD] = part.T.astype(BF16)


SIDES = (
    dict(give=(1, 3), keep=(0, 3), last=1),
    dict(give=(2, 4), keep=(1, 0), last=0),
)


def owner_of(offset, side):
    h = lax.axis_index("head")
    x, z = h // 4, lax.rem(h, 4)
    if offset == 0:
        oz = z
    elif offset == 1:
        oz = z + 1 - 2 * lax.rem(z, 2)
    elif offset == 2:
        oz = lax.rem(z + 2, 4)
    else:
        oz = 3 - z
    ox = x if side == 0 else 1 - x
    return ox * 4 + oz


WEIGHT_ORDER = (2, 1, 3, 0)


def weight_copies(offsets, w_q, w_k, w_v, w, sem):
    for offset in offsets:
        for side in range(2):
            rows = pl.ds(pl.multiple_of(owner_of(offset, side) * COLS, COLS), COLS)
            into = pl.ds(side * COLS, COLS)
            yield from [
                pltpu.make_async_copy(w_q.at[rows], w.at[offset, into, pl.ds(0, 1024)], sem.at[offset, side, 0]),
                pltpu.make_async_copy(w_k.at[rows], w.at[offset, into, pl.ds(1024, HD)], sem.at[offset, side, 1]),
                pltpu.make_async_copy(w_v.at[rows], w.at[offset, into, pl.ds(1152, HD)], sem.at[offset, side, 2]),
            ]


class HeadSum:
    def __init__(self, chunk, terms, r1, s2, r2, s3, r3, sems):
        self.chunk = chunk
        self.terms, self.r1, self.s2, self.r2, self.s3, self.r3 = (
            terms.at[chunk], r1.at[chunk], s2.at[chunk], r2.at[chunk], s3.at[chunk], r3.at[chunk]
        )
        self.sems = sems
        self.seq = lax.axis_index("seq")
        self.z1, self.z3, self.flip = head_peers()

    def copy(self, half, step):
        send, recv = (self.sems.at[k, self.chunk, half, step] for k in range(2))
        near, far = (self.z1, self.z3) if half == 0 else (self.z3, self.z1)
        if step == 0:
            low, high = SIDES[half]["give"]
            src = self.terms.at[pl.ds(low, high - low), :, pl.ds(half * 64, 64), :]
            return remote(src, self.r1.at[half], send, recv, self.seq, near)
        if step == 1:
            return remote(self.s2.at[half], self.r2.at[half], send, recv, self.seq, self.flip)
        return remote(self.s3.at[half], self.r3.at[half], send, recv, self.seq, far)

    def first(self, half):
        self.copy(half, 0).start()

    def second(self, half):
        self.copy(half, 0).wait_recv()
        rows = slice(half * 64, half * 64 + 64)
        for k, offset in enumerate(SIDES[half]["keep"]):
            total = self.terms[offset, 1, rows, :].astype(F32) + self.r1[half, k, 1].astype(F32)
            self.s2[half, k] = total.astype(BF16)
        self.copy(half, 1).start()

    def kept(self, half, k):
        rows = slice(half * 64, half * 64 + 64)
        offset = SIDES[half]["keep"][k]
        return (
            self.terms[offset, 0, rows, :].astype(F32)
            + self.r1[half, k, 0].astype(F32)
            + self.r2[half, k].astype(F32)
        )

    def third(self, half):
        self.copy(half, 1).wait_recv()
        self.s3[half] = self.kept(half, SIDES[half]["last"]).astype(BF16)
        self.copy(half, 2).start()

    def final(self, half, out, base):
        total = self.kept(half, 1 - SIDES[half]["last"])
        self.copy(half, 2).wait_recv()
        out[base + half * 64 : base + half * 64 + 64, :] = (
            total + self.r3[half].astype(F32)
        ).astype(BF16)

    def drain(self):
        for half in range(2):
            for step in range(3):
                self.copy(half, step).wait_send()


def store_terms(block, terms, chunk, offset, part):
    for piece in range(2):
        side, lane = divmod(part * 256 + piece * 128, COLS)
        terms[chunk, offset, side, :, lane : lane + 128] = block[:, piece * 128 : piece * 128 + 128]


def project(d, w, terms, chunk, wait_weights):
    rows = d[...]
    for offset in WEIGHT_ORDER:
        if wait_weights is not None:
            wait_weights(offset)
        for part in range(5):
            block = dot(rows, w[offset, part * 256 : (part + 1) * 256, :], NT)
            store_terms(block.astype(BF16), terms, chunk, offset, part)


def project_early(d, w, early):
    rows = d[:, :1024]
    for offset in WEIGHT_ORDER:
        for part in range(5):
            cols = slice(part * 256, (part + 1) * 256)
            early[offset, :, cols] = dot(rows, w[offset, cols, :1024], NT)


def project_late(d, w, early, terms, chunk):
    rows = d[:, 1024:]
    for offset in WEIGHT_ORDER:
        for part in range(5):
            cols = slice(part * 256, (part + 1) * 256)
            block = early[offset, :, cols] + dot(rows, w[offset, cols, 1024:], NT)
            store_terms(block.astype(BF16), terms, chunk, offset, part)


def grads_sibling(grads, rc, gsem):
    c = lax.rem(lax.axis_index("seq"), 2)
    return remote(
        grads.at[:, 1 - c], rc, gsem.at[0, 7], gsem.at[1, 7], seq_sibling(), lax.axis_index("head")
    )


def grads_copies(gs, rg, gsem):
    y, x, c = seq_place()
    copies = []
    for j, (dy, dx) in enumerate(SEQ_STEPS):
        oy = lax.rem(y + dy, 4)
        ox = lax.rem(x + dx, 2)
        block = lax.rem(oy, 2) * 2 + ox
        copies.append(
            remote(
                gs.at[block, oy // 2], rg.at[j], gsem.at[0, j], gsem.at[1, j],
                seq_peer(dy, dx), lax.axis_index("head"),
            )
        )
    return copies


def grads_second(grads, rc, gs, rg, gsem):
    c = lax.rem(lax.axis_index("seq"), 2)
    grads_sibling(grads, rc, gsem).wait_recv()
    for b in range(4):
        for p in range(2):
            gs[b, p] = (grads[b, c, p].astype(F32) + rc[b, p].astype(F32)).astype(BF16)
    for copy in grads_copies(gs, rg, gsem):
        copy.start()


def grads_finish(gs, rg, gsem, d_p):
    y, x, c = seq_place()
    total = gs[lax.rem(y, 2) * 2 + x, y // 2].astype(F32)
    for j, copy in enumerate(grads_copies(gs, rg, gsem)):
        copy.wait_recv()
        total = total + rg[j].astype(F32)
    d_p[:, 1024:] = total.astype(BF16)


def whole_kernel(
    lens_ref, prompt_ref, q_p_h, k_p_h, v_p_h, do_p_h, q_r_h, k_r_h, v_r_h, do_r_h, w_q, w_k, w_v,
    out_p, out_r,
    kv, q_p, do_p, q_r, do_r, k_r, v_r,
    kke, vve, kket, qext, doext, s_ref, dp_ref, et, dst, dkk, dvv, bias, d_r, d_p, grads, early,
    w, terms, r1, s2, r2, s3, r3, rc, gs, rg,
    lsem, send, recv, fsend, frecv, wsem, hsem, gsem,
):
    seq, head = lax.axis_index("seq"), lax.axis_index("head")
    barrier = pltpu.get_barrier_semaphore()
    seqs = [seq_sibling()] + [seq_peer(dy, dx) for dy, dx in SEQ_STEPS]
    heads = list(head_peers())
    for peer in seqs:
        pl.semaphore_signal(barrier, inc=1, device_id=(peer, head), device_id_type=MESH)
    for peer in heads:
        pl.semaphore_signal(barrier, inc=1, device_id=(seq, peer), device_id_type=MESH)
    loads = [
        pltpu.make_async_copy(src, dst_ref, lsem.at[k])
        for k, (src, dst_ref) in enumerate((
            (k_p_h, kv.at[seq, 0]), (v_p_h, kv.at[seq, 1]), (q_r_h, q_r), (do_r_h, do_r),
            (k_r_h, k_r), (v_r_h, v_r), (q_p_h, q_p), (do_p_h, do_p),
        ))
    ]
    for copy in loads:
        copy.start()
    for copy in loads[:2]:
        copy.wait()
    pl.semaphore_wait(barrier, len(seqs) + len(heads))
    gather_start(kv, send, recv, fsend, frecv)
    for copy in weight_copies(WEIGHT_ORDER, w_q, w_k, w_v, w, wsem):
        copy.start()
    for copy in loads[2:]:
        copy.wait()
    sums = [HeadSum(c, terms, r1, s2, r2, s3, r3, hsem) for c in range(3)]

    def response(half, first):
        tiles = 8 + half + 1
        count = (half + 1) * TOK
        base = half * TOK
        col = base + lax.broadcasted_iota(jnp.int32, (TOK, 1), 0)
        col_prompt = prompt_of(segment_of(col, lens_ref), prompt_ref)
        row = base + lax.rem(lax.broadcasted_iota(jnp.int32, (1, 256), 1), TOK)
        row_seg = segment_of(row, lens_ref)
        row_prompt = prompt_of(row_seg[:, :TOK], prompt_ref)
        key = lax.broadcasted_iota(jnp.int32, (count, 1), 0)
        key_seg = segment_of(key, lens_ref)
        seen = (key_seg == row_seg) & (key <= row)
        bias[:count, :] = jnp.where(seen, 0.0, NEG)
        span = slice(base, base + TOK)
        load_rows(q_r.at[span], do_r.at[span], col_prompt, qext, doext)
        if first:
            gather_finish(kv, send, recv, fsend, frecv)
            load_keys(kv, k_r, v_r, kke, vve, kket)

        def local_bias(t, s):
            if t < 8:
                return s
            return s + bias[(t - 8) * TOK : (t - 7) * TOK, :]

        def visit(hp, c):
            head_pair(
                hp, tiles, local_bias, qext, doext, kke, vve, s_ref, dp_ref, et, dst
            )
            return c

        lax.fori_loop(0, 4, visit, 0)
        chunk_products(tiles, first, qext, doext, kket, et, dst, dkk, dvv)
        chunk_dq(tiles, row_prompt, kket, dst, d_r, span)
        local = slice(1024 + base, 1024 + base + TOK)
        d_r[span, 1024:1152] = ((dkk[local, :HD] + dkk[local, HD:]) * SCALE).astype(BF16)
        d_r[span, 1152:] = (dvv[local, :HD] + dvv[local, HD:]).astype(BF16)

    def wait_weights(offset):
        for copy in weight_copies((offset,), w_q, w_k, w_v, w, wsem):
            copy.wait()

    def both(step, chunk):
        for half in range(2):
            step(sums[chunk], half)

    response(1, True)
    project(d_r.at[TOK:256], w, terms, 1, wait_weights)
    both(HeadSum.first, 1)
    response(0, False)
    both(HeadSum.second, 1)

    place = lax.rem(seq, 8) * TOK
    diff = (
        place
        + lax.rem(lax.broadcasted_iota(jnp.int32, (TOK, 256), 1), TOK)
        - lax.broadcasted_iota(jnp.int32, (TOK, 256), 0)
    )
    mine = seq // 8
    load_rows(q_p, do_p, jnp.full((TOK, 1), mine, jnp.int32), qext, doext)

    def causal(t, s):
        return jnp.where(diff >= t * TOK, s, NEG)

    def visit(hp, c):
        head_pair(hp, 8, causal, qext, doext, kke, vve, s_ref, dp_ref, et, dst)
        return c

    lax.fori_loop(0, 4, visit, 0)
    chunk_products(8, False, qext, doext, kket, et, dst, dkk, dvv)
    for r in range(8):
        keys = slice(r * TOK, (r + 1) * TOK)
        for p in range(2):
            lanes = slice(p * HD, (p + 1) * HD)
            grads[r // 2, r % 2, p, :, :HD] = (dkk[keys, lanes] * SCALE).astype(BF16)
            grads[r // 2, r % 2, p, :, HD:] = dvv[keys, lanes].astype(BF16)
    grads_sibling(grads, rc, gsem).start()
    both(HeadSum.third, 1)
    chunk_dq(8, jnp.full((1, TOK), mine, jnp.int32), kket, dst, d_p, slice(0, TOK))
    grads_second(grads, rc, gs, rg, gsem)
    project(d_r.at[0:TOK], w, terms, 0, None)
    both(HeadSum.first, 0)
    project_early(d_p, w, early)
    both(HeadSum.second, 0)
    grads_finish(gs, rg, gsem, d_p)
    project_late(d_p, w, early, terms, 2)
    both(HeadSum.first, 2)
    both(HeadSum.third, 0)
    for half in range(2):
        sums[1].final(half, out_r, TOK)
    both(HeadSum.second, 2)
    for half in range(2):
        sums[0].final(half, out_r, 0)
    both(HeadSum.third, 2)
    for half in range(2):
        sums[2].final(half, out_p, 0)
    grads_sibling(grads, rc, gsem).wait_send()
    for copy in grads_copies(gs, rg, gsem):
        copy.wait_send()
    for c in range(3):
        sums[c].drain()


def shards(
    q_prompt, k_prompt, v_prompt, do_prompt, q_resp, k_resp, v_resp, do_resp,
    resp_lengths, resp_prompt, w_query, w_key, w_value,
):
    whole = pl.BlockSpec(memory_space=VMEM)
    hbm = pl.BlockSpec(memory_space=pl.ANY)
    scalars = pl.BlockSpec(memory_space=pltpu.SMEM)
    return pl.pallas_call(
        whole_kernel,
        out_shape=(
            jax.ShapeDtypeStruct((TOK, COLS), BF16),
            jax.ShapeDtypeStruct((256, COLS), BF16),
        ),
        in_specs=[scalars] * 2 + [hbm] * 11,
        out_specs=(whole,) * 2,
        scratch_shapes=[
            VMEM((16, 2, TOK, HD), BF16),
            VMEM((TOK, 1024), BF16),
            VMEM((TOK, 1024), BF16),
            VMEM((256, 1024), BF16),
            VMEM((256, 1024), BF16),
            VMEM((256, HD), BF16),
            VMEM((256, HD), BF16),
            VMEM((WIDE, 256), BF16),
            VMEM((WIDE, 256), BF16),
            VMEM((256, WIDE), BF16),
            VMEM((1024, 256), BF16),
            VMEM((1024, 256), BF16),
            VMEM((WIDE, 256), F32),
            VMEM((WIDE, 256), F32),
            VMEM((WIDE, 1024), BF16),
            VMEM((WIDE, 1024), BF16),
            VMEM((WIDE, 256), F32),
            VMEM((WIDE, 256), F32),
            VMEM((256, 256), F32),
            VMEM((256, WIDE), BF16),
            VMEM((TOK, WIDE), BF16),
            VMEM((4, 2, 2, TOK, 256), BF16),
            VMEM((4, TOK, WIDE), F32),
            VMEM((4, WIDE, WIDE), BF16),
            VMEM((3, 4, 2, TOK, COLS), BF16),
            VMEM((3, 2, 2, 2, 64, COLS), BF16),
            VMEM((3, 2, 2, 64, COLS), BF16),
            VMEM((3, 2, 2, 64, COLS), BF16),
            VMEM((3, 2, 64, COLS), BF16),
            VMEM((3, 2, 64, COLS), BF16),
            VMEM((4, 2, TOK, 256), BF16),
            VMEM((4, 2, TOK, 256), BF16),
            VMEM((7, TOK, 256), BF16),
            pltpu.SemaphoreType.DMA((8,)),
            pltpu.SemaphoreType.DMA((7,)),
            pltpu.SemaphoreType.DMA((7,)),
            pltpu.SemaphoreType.DMA((8,)),
            pltpu.SemaphoreType.DMA((8,)),
            pltpu.SemaphoreType.DMA((4, 2, 3)),
            pltpu.SemaphoreType.DMA((2, 3, 2, 3)),
            pltpu.SemaphoreType.DMA((2, 8)),
        ],
        compiler_params=pltpu.CompilerParams(
            collective_id=0, has_side_effects=True, vmem_limit_bytes=60 << 20
        ),
        name="attention_back",
    )(
        resp_lengths, resp_prompt, q_prompt, k_prompt, v_prompt, do_prompt,
        q_resp, k_resp, v_resp, do_resp, w_query, w_key, w_value,
    )


def solution(mesh):
    return jax.shard_map(
        shards,
        mesh=mesh,
        in_specs=(P("seq", "head"),) * 8 + (P("seq", None),) * 2 + (P(None, "head"),) * 3,
        out_specs=(P("seq", "head"), P("seq", "head")),
        check_vma=False,
    )
```

```python
import functools
import math

import jax
import jax.numpy as jnp
from jax import lax
from jax.experimental import pallas as pl
from jax.experimental.pallas import tpu as pltpu
from jax.sharding import PartitionSpec as P

MESH = pl.DeviceIdType.MESH
VMEM = pltpu.VMEM
BF16 = jnp.bfloat16
F32 = jnp.float32
HD = 128
GROUP = 8
TOK = 128
NEG = -1e30
SCALE = 1.0 / math.sqrt(HD)
EXP2 = SCALE * math.log2(math.e)
D = 5120
COLS = 640
HALF = 320
WIDE = 1280
NT = (((1,), (1,)), ((), ()))
NN = (((1,), (0,)), ((), ()))


def dot(a, b, dims):
    return lax.dot_general(a, b, dims, preferred_element_type=F32)


def remote(src, dst, send, recv, seq, head):
    return pltpu.make_async_remote_copy(
        src_ref=src, dst_ref=dst, send_sem=send, recv_sem=recv,
        device_id=(seq, head), device_id_type=MESH,
    )


def seq_place():
    n = lax.axis_index("seq")
    return n // 4, lax.rem(n // 2, 2), lax.rem(n, 2)


def seq_peer(dy, dx):
    y, x, c = seq_place()
    return lax.rem(y + dy + 4, 4) * 4 + lax.rem(x + dx, 2) * 2 + c


def seq_sibling():
    n = lax.axis_index("seq")
    return n + 1 - 2 * lax.rem(n, 2)


SEQ_STEPS = [(0, 1), (1, 0), (3, 0), (1, 1), (3, 1), (2, 0), (2, 1)]


def head_peers():
    h = lax.axis_index("head")
    x, z = h // 4, lax.rem(h, 4)
    base = x * 4
    z1 = base + z + 1 - 2 * lax.rem(z, 2)
    z3 = base + 3 - z
    flip = (1 - x) * 4 + z
    return z1, z3, flip


def gather_copies(kv, send, recv, fsend, frecv):
    n, head = lax.axis_index("seq"), lax.axis_index("head")
    sib = seq_sibling()
    firsts = [remote(kv.at[n], kv.at[n], fsend.at[0], frecv.at[0], sib, head)]
    for j, (dy, dx) in enumerate(SEQ_STEPS):
        firsts.append(
            remote(kv.at[n], kv.at[n], send.at[j], recv.at[j], seq_peer(dy, dx), head)
        )
    return firsts


def gather_start(kv, send, recv, fsend, frecv):
    for copy in gather_copies(kv, send, recv, fsend, frecv):
        copy.start()


def gather_finish(kv, send, recv, fsend, frecv):
    head = lax.axis_index("head")
    sib = seq_sibling()
    firsts = gather_copies(kv, send, recv, fsend, frecv)
    forwards = []
    for j, (dy, dx) in enumerate(SEQ_STEPS):
        src = seq_peer(-dy, dx)
        firsts[j + 1].wait_recv()
        forward = remote(kv.at[src], kv.at[src], fsend.at[j + 1], frecv.at[j + 1], sib, head)
        forward.start()
        forwards.append(forward)
    for copy in [firsts[0]] + forwards:
        copy.wait_recv()
    for copy in firsts + forwards:
        copy.wait_send()


def segment_of(place, lens_ref):
    end = jnp.int32(0)
    seg = jnp.zeros(place.shape, jnp.int32)
    for c in range(4):
        end = end + lens_ref[0, c]
        seg = seg + (place >= end).astype(jnp.int32)
    return seg


def prompt_of(seg, prompt_ref):
    out = jnp.zeros(seg.shape, jnp.int32)
    for c in range(4):
        out = jnp.where(seg == c, prompt_ref[0, c], out)
    return out


def load_keys(kv, k_r, v_r, kke, vve):
    for r in range(8):
        rows = pl.ds(r * TOK, TOK)
        kke[rows, :HD] = kv[r, 0]
        kke[rows, HD:] = kv[8 + r, 0]
        vve[rows, :HD] = kv[r, 1]
        vve[rows, HD:] = kv[8 + r, 1]
    local = pl.ds(1024, 256)
    kke[local, :HD] = k_r[...]
    kke[local, HD:] = k_r[...]
    vve[local, :HD] = v_r[...]
    vve[local, HD:] = v_r[...]


def turn_keys(kke, kket):
    for r in range(10):
        rows = pl.ds(r * TOK, TOK)
        kket[:, rows] = kke[rows, :].T


def load_rows(q, do, col_prompt, qext, doext):
    first = col_prompt == 0
    zero = jnp.zeros((TOK, HD), BF16)
    first = jnp.broadcast_to(first, (TOK, HD))
    for h in range(GROUP):
        lanes = pl.ds(h * HD, HD)
        rows = pl.ds(h * TOK, TOK)
        qv, dov = q[:, lanes], do[:, lanes]
        qext[rows, :HD] = jnp.where(first, qv, zero)
        qext[rows, HD:] = jnp.where(first, zero, qv)
        doext[rows, :HD] = jnp.where(first, dov, zero)
        doext[rows, HD:] = jnp.where(first, zero, dov)


def fold(x, op):
    return op(x.reshape(x.shape[0] // 8, 8, x.shape[1]), axis=0)


def key_groups(keys):
    size = 256
    return [(k, min(size, keys - k)) for k in range(0, keys, size)]


def chunk_scores(keys, bias_of, qext, doext, kke, vve, s_refs, dp_refs, et, dst):
    low = jnp.full((8, 256), NEG, F32)

    def scores(hp, group, top):
        start, size = group
        s = dot(kke[start : start + size, :], qext[hp * 256 : hp * 256 + 256, :], NT)
        for j in range(0, size, TOK):
            tile = bias_of((start + j) // TOK, s[j : j + TOK])
            s_refs[hp % 2][start + j : start + j + TOK, :] = tile
            top = jnp.maximum(top, fold(tile, jnp.max))
        return top

    def grads(hp, group):
        span = slice(group[0], group[0] + group[1])
        dp_refs[hp % 2][span, :] = dot(vve[span, :], doext[hp * 256 : hp * 256 + 256, :], NT)

    def tiles(group):
        return [slice(j, j + TOK) for j in range(group[0], group[0] + group[1], TOK)]

    groups = key_groups(keys)
    top = low
    for group in groups:
        top = scores(0, group, top)
        grads(0, group)
    for hp in range(4):
        s_ref, dp_ref = s_refs[hp % 2], dp_refs[hp % 2]
        cols = slice(hp * 256, hp * 256 + 256)
        top = jnp.max(top, axis=0, keepdims=True)
        norm = jnp.zeros((8, 256), F32)
        weighted = jnp.zeros((8, 256), F32)
        next_top = low
        for group in groups:
            if hp < 3:
                next_top = scores(hp + 1, group, next_top)
            for span in tiles(group):
                e = jnp.exp2((s_ref[span, :] - top) * EXP2)
                s_ref[span, :] = e
                norm = norm + fold(e, jnp.sum)
                weighted = weighted + fold(e * dp_ref[span, :], jnp.sum)
        inv = 1.0 / jnp.sum(norm, axis=0, keepdims=True)
        mean = jnp.sum(weighted, axis=0, keepdims=True) * inv
        for group in groups:
            if hp < 3:
                grads(hp + 1, group)
            for span in tiles(group):
                p = s_ref[span, :] * inv
                et[span, cols] = p.astype(BF16)
                dst[span, cols] = (p * (dp_ref[span, :] - mean)).astype(BF16)
        top = next_top


def chunk_product(keys, first, left, right, total):
    for start, size in key_groups(keys):
        span = slice(start, start + size)
        value = dot(left[span, :], right[...], NN)
        if first:
            total[span, :] = value
        else:
            total[span, :] += value


def chunk_dq(keys, row_prompt, kket, dst, dq_ref, rows_out):
    first = row_prompt == 0
    for hp in range(4):
        both = dot(kket[:, :keys], dst[:keys, hp * 256 : hp * 256 + 256], NN)
        for k in range(2):
            lanes = slice(k * TOK, (k + 1) * TOK)
            part = jnp.where(first, both[:HD, lanes], both[HD:, lanes]) * SCALE
            h = hp * 2 + k
            dq_ref[rows_out, h * HD : (h + 1) * HD] = part.T.astype(BF16)


SIDES = (
    dict(give=(1, 3), keep=(0, 3), last=1),
    dict(give=(2, 4), keep=(1, 0), last=0),
)


def owner_of(offset, side):
    h = lax.axis_index("head")
    x, z = h // 4, lax.rem(h, 4)
    if offset == 0:
        oz = z
    elif offset == 1:
        oz = z + 1 - 2 * lax.rem(z, 2)
    elif offset == 2:
        oz = lax.rem(z + 2, 4)
    else:
        oz = 3 - z
    ox = x if side == 0 else 1 - x
    return ox * 4 + oz


WEIGHT_ORDER = (2, 1, 3, 0)


def weight_copies(offsets, w_q, w_k, w_v, w, sem):
    for offset in offsets:
        for side in range(2):
            rows = pl.ds(pl.multiple_of(owner_of(offset, side) * COLS, COLS), COLS)
            into = pl.ds(side * COLS, COLS)
            yield from [
                pltpu.make_async_copy(w_q.at[rows], w.at[offset, into, pl.ds(0, 1024)], sem.at[offset, side, 0]),
                pltpu.make_async_copy(w_k.at[rows], w.at[offset, into, pl.ds(1024, HD)], sem.at[offset, side, 1]),
                pltpu.make_async_copy(w_v.at[rows], w.at[offset, into, pl.ds(1152, HD)], sem.at[offset, side, 2]),
            ]


class HeadSum:
    def __init__(self, chunk, terms, r1, s2, r2, s3, r3, sums, sems):
        self.chunk = chunk
        self.terms, self.r1, self.s2, self.r2, self.s3, self.r3 = (
            terms.at[chunk], r1.at[chunk], s2.at[chunk], r2.at[chunk], s3.at[chunk], r3.at[chunk]
        )
        self.sums = sums.at[chunk]
        self.sems = sems
        self.seq = lax.axis_index("seq")
        self.z1, self.z3, self.flip = head_peers()

    def copy(self, half, step):
        send, recv = (self.sems.at[k, self.chunk, half, step] for k in range(2))
        near, far = (self.z1, self.z3) if half == 0 else (self.z3, self.z1)
        if step < 2:
            side = 1 - step
            low, high = SIDES[half]["give"]
            src = self.terms.at[pl.ds(low, high - low), half, side]
            return remote(src, self.r1.at[half, side], send, recv, self.seq, near)
        if step < 4:
            k = step - 2
            return remote(self.s2.at[half, k], self.r2.at[half, k], send, recv, self.seq, self.flip)
        return remote(self.s3.at[half], self.r3.at[half], send, recv, self.seq, far)

    def first(self, half):
        self.copy(half, 0).start()
        self.copy(half, 1).start()

    def second(self, half):
        self.copy(half, 0).wait_recv()
        last = SIDES[half]["last"]
        for k in (last, 1 - last):
            offset = SIDES[half]["keep"][k]
            total = self.terms[offset, half, 1].astype(F32) + self.r1[half, 1, k].astype(F32)
            self.s2[half, k] = total.astype(BF16)
            self.copy(half, 2 + k).start()

    def kept(self, half, k):
        self.copy(half, 2 + k).wait_recv()
        offset = SIDES[half]["keep"][k]
        return (
            self.terms[offset, half, 0].astype(F32)
            + self.r1[half, 0, k].astype(F32)
            + self.r2[half, k].astype(F32)
        )

    def third(self, half):
        self.copy(half, 1).wait_recv()
        self.s3[half] = self.kept(half, SIDES[half]["last"]).astype(BF16)
        self.copy(half, 4).start()

    def final(self, half):
        total = self.kept(half, 1 - SIDES[half]["last"])
        self.copy(half, 4).wait_recv()
        self.sums[half * HALF : (half + 1) * HALF, :] = total + self.r3[half].astype(F32)

    def write(self, out, base):
        for part in range(5):
            lanes = slice(part * TOK, (part + 1) * TOK)
            out[base : base + TOK, lanes] = self.sums[lanes, :].T.astype(BF16)

    def drain(self):
        for half in range(2):
            for step in range(5):
                self.copy(half, step).wait_send()


BLOCKS = ((1, 0), (1, 1), (0, 0), (0, 1))


def block_rows(side, half):
    start = side * COLS + half * HALF
    return slice(start, start + HALF)


def project(rows, w, put, wait_weights, started):
    for offset in WEIGHT_ORDER:
        if wait_weights is not None:
            wait_weights(offset)
        for side, half in BLOCKS:
            put(offset, half, side, dot(w[offset, block_rows(side, half), :], rows, NT))
        if offset in started:
            started[offset]()


def grads_sibling(grads, rc, gsem):
    c = lax.rem(lax.axis_index("seq"), 2)
    return remote(
        grads.at[:, 1 - c], rc, gsem.at[0, 7], gsem.at[1, 7], seq_sibling(), lax.axis_index("head")
    )


def grads_copies(gs, rg, gsem):
    y, x, c = seq_place()
    copies = []
    for j, (dy, dx) in enumerate(SEQ_STEPS):
        oy = lax.rem(y + dy, 4)
        ox = lax.rem(x + dx, 2)
        block = lax.rem(oy, 2) * 2 + ox
        copies.append(
            remote(
                gs.at[block, oy // 2], rg.at[j], gsem.at[0, j], gsem.at[1, j],
                seq_peer(dy, dx), lax.axis_index("head"),
            )
        )
    return copies


def grads_second(grads, rc, gs, rg, gsem):
    c = lax.rem(lax.axis_index("seq"), 2)
    grads_sibling(grads, rc, gsem).wait_recv()
    for b in range(4):
        for p in range(2):
            gs[b, p] = (grads[b, c, p].astype(F32) + rc[b, p].astype(F32)).astype(BF16)
    for copy in grads_copies(gs, rg, gsem):
        copy.start()


def grads_finish(gs, rg, gsem, d_p):
    y, x, c = seq_place()
    total = gs[lax.rem(y, 2) * 2 + x, y // 2].astype(F32)
    for j, copy in enumerate(grads_copies(gs, rg, gsem)):
        copy.wait_recv()
        total = total + rg[j].astype(F32)
    d_p[...] = total.astype(BF16)


def whole_kernel(
    lens_ref, prompt_ref, q_p_h, k_p_h, v_p_h, do_p_h, q_r_h, k_r_h, v_r_h, do_r_h, w_q, w_k, w_v,
    out_p, out_r,
    kv, q_p, do_p, q_r, do_r, k_r, v_r,
    kke, vve, kket, qext, doext, s0, s1, dp0, dp1, et, dst, dkk, dvv, bias0, bias1, d_b, d_ap, late, grads, early,
    w, terms, r1, s2, r2, s3, r3, totals, rc, gs, rg,
    lsem, send, recv, fsend, frecv, wsem, hsem, gsem,
):
    seq, head = lax.axis_index("seq"), lax.axis_index("head")
    barrier = pltpu.get_barrier_semaphore()
    seqs = [seq_sibling()] + [seq_peer(dy, dx) for dy, dx in SEQ_STEPS]
    heads = list(head_peers())
    for peer in seqs:
        pl.semaphore_signal(barrier, inc=1, device_id=(peer, head), device_id_type=MESH)
    for peer in heads:
        pl.semaphore_signal(barrier, inc=1, device_id=(seq, peer), device_id_type=MESH)
    loads = [
        pltpu.make_async_copy(src, dst_ref, lsem.at[k])
        for k, (src, dst_ref) in enumerate((
            (k_p_h, kv.at[seq, 0]), (v_p_h, kv.at[seq, 1]), (q_r_h, q_r), (do_r_h, do_r),
            (k_r_h, k_r), (v_r_h, v_r), (q_p_h, q_p), (do_p_h, do_p),
        ))
    ]
    for copy in loads:
        copy.start()
    for copy in loads[:2]:
        copy.wait()
    pl.semaphore_wait(barrier, len(seqs) + len(heads))
    gather_start(kv, send, recv, fsend, frecv)
    for copy in weight_copies(WEIGHT_ORDER, w_q, w_k, w_v, w, wsem):
        copy.start()
    for copy in loads[2:]:
        copy.wait()
    sums = [HeadSum(c, terms, r1, s2, r2, s3, r3, totals, hsem) for c in range(3)]
    mine = seq // 8

    row_prompts = []
    for half, bias in ((0, bias0), (1, bias1)):
        base = half * TOK
        col = base + lax.broadcasted_iota(jnp.int32, (TOK, 1), 0)
        row = base + lax.rem(lax.broadcasted_iota(jnp.int32, (1, 256), 1), TOK)
        row_seg = segment_of(row, lens_ref)
        row_prompts.append(prompt_of(row_seg[:, :TOK], prompt_ref))
        key = lax.broadcasted_iota(jnp.int32, (base + TOK, 1), 0)
        key_seg = segment_of(key, lens_ref)
        seen = (key_seg == row_seg) & (key <= row)
        bias[...] = jnp.where(seen, 0.0, NEG)
        span = slice(base, base + TOK)
        load_rows(
            q_r.at[span], do_r.at[span], prompt_of(segment_of(col, lens_ref), prompt_ref),
            qext.at[half], doext.at[half],
        )
    load_rows(q_p, do_p, jnp.full((TOK, 1), mine, jnp.int32), qext.at[2], doext.at[2])
    diff = (
        lax.rem(seq, 8) * TOK
        + lax.rem(lax.broadcasted_iota(jnp.int32, (TOK, 256), 1), TOK)
        - lax.broadcasted_iota(jnp.int32, (TOK, 256), 0)
    )
    d_ap[TOK:, 1024:] = jnp.zeros((TOK, 256), BF16)
    gather_finish(kv, send, recv, fsend, frecv)
    load_keys(kv, k_r, v_r, kke, vve)

    def scores(keys, bias_of, chunk):
        chunk_scores(
            keys, bias_of, qext.at[chunk], doext.at[chunk], kke, vve, (s0, s1), (dp0, dp1), et, dst
        )

    def response(half, first, d_ref):
        bias = (bias0, bias1)[half]
        keys = 1024 + (half + 1) * TOK

        def local_bias(t, s):
            if t < 8:
                return s
            return s + bias[(t - 8) * TOK : (t - 7) * TOK, :]

        scores(keys, local_bias, half)
        if first:
            turn_keys(kke, kket)
        chunk_product(keys, first, et, doext.at[half], dvv)
        chunk_product(keys, first, dst, qext.at[half], dkk)
        chunk_dq(keys, row_prompts[half], kket, dst, d_ref, slice(0, TOK))
        local = slice(1024 + half * TOK, 1024 + half * TOK + TOK)
        d_ref[:TOK, 1024:1152] = ((dkk[local, :HD] + dkk[local, HD:]) * SCALE).astype(BF16)
        d_ref[:TOK, 1152:] = (dvv[local, :HD] + dvv[local, HD:]).astype(BF16)

    def wait_weights(offset):
        for copy in weight_copies((offset,), w_q, w_k, w_v, w, wsem):
            copy.wait()

    def both(step, chunk):
        for half in range(2):
            step(sums[chunk], half)

    def starts(chunk):
        return {1: lambda: sums[chunk].first(0), 3: lambda: sums[chunk].first(1)}

    def put_b(offset, half, side, value):
        terms[1, offset, half, side] = value.astype(BF16)

    def put_ap(offset, half, side, value):
        terms[0, offset, half, side] = value[:, :TOK].astype(BF16)
        early[offset, half, side] = value[:, TOK:]

    response(1, True, d_b)
    project(d_b[...], w, put_b, wait_weights, starts(1))
    response(0, False, d_ap)
    both(HeadSum.second, 1)

    scores(1024, lambda t, s: jnp.where(diff >= t * TOK, s, NEG), 2)
    chunk_product(1024, False, et, doext.at[2], dvv)
    chunk_product(1024, False, dst, qext.at[2], dkk)
    for r in range(8):
        keys = slice(r * TOK, (r + 1) * TOK)
        for p in range(2):
            lanes = slice(p * HD, (p + 1) * HD)
            grads[r // 2, r % 2, p, :, :HD] = (dkk[keys, lanes] * SCALE).astype(BF16)
            grads[r // 2, r % 2, p, :, HD:] = dvv[keys, lanes].astype(BF16)
    grads_sibling(grads, rc, gsem).start()
    chunk_dq(1024, jnp.full((1, TOK), mine, jnp.int32), kket, dst, d_ap, slice(TOK, 256))
    both(HeadSum.third, 1)
    grads_second(grads, rc, gs, rg, gsem)
    project(d_ap[...], w, put_ap, None, starts(0))
    both(HeadSum.final, 1)
    sums[1].write(out_r, TOK)
    both(HeadSum.second, 0)
    grads_finish(gs, rg, gsem, late)
    rows = late[...]
    for offset in WEIGHT_ORDER:
        for side, half in BLOCKS:
            value = dot(w[offset, block_rows(side, half), 1024:], rows, NT)
            terms[2, offset, half, side] = (early[offset, half, side] + value).astype(BF16)
        if offset in (1, 3):
            starts(2)[offset]()
    both(HeadSum.third, 0)
    both(HeadSum.second, 2)
    both(HeadSum.final, 0)
    sums[0].write(out_r, 0)
    both(HeadSum.third, 2)
    both(HeadSum.final, 2)
    sums[2].write(out_p, 0)
    grads_sibling(grads, rc, gsem).wait_send()
    for copy in grads_copies(gs, rg, gsem):
        copy.wait_send()
    for c in range(3):
        sums[c].drain()


def shards(
    q_prompt, k_prompt, v_prompt, do_prompt, q_resp, k_resp, v_resp, do_resp,
    resp_lengths, resp_prompt, w_query, w_key, w_value,
):
    whole = pl.BlockSpec(memory_space=VMEM)
    hbm = pl.BlockSpec(memory_space=pl.ANY)
    scalars = pl.BlockSpec(memory_space=pltpu.SMEM)
    return pl.pallas_call(
        whole_kernel,
        out_shape=(
            jax.ShapeDtypeStruct((TOK, COLS), BF16),
            jax.ShapeDtypeStruct((256, COLS), BF16),
        ),
        in_specs=[scalars] * 2 + [hbm] * 11,
        out_specs=(whole,) * 2,
        scratch_shapes=[
            VMEM((16, 2, TOK, HD), BF16),
            VMEM((TOK, 1024), BF16),
            VMEM((TOK, 1024), BF16),
            VMEM((256, 1024), BF16),
            VMEM((256, 1024), BF16),
            VMEM((256, HD), BF16),
            VMEM((256, HD), BF16),
            VMEM((WIDE, 256), BF16),
            VMEM((WIDE, 256), BF16),
            VMEM((256, WIDE), BF16),
            VMEM((3, 1024, 256), BF16),
            VMEM((3, 1024, 256), BF16),
            VMEM((WIDE, 256), F32),
            VMEM((WIDE, 256), F32),
            VMEM((WIDE, 256), F32),
            VMEM((WIDE, 256), F32),
            VMEM((WIDE, 1024), BF16),
            VMEM((WIDE, 1024), BF16),
            VMEM((WIDE, 256), F32),
            VMEM((WIDE, 256), F32),
            VMEM((TOK, 256), F32),
            VMEM((256, 256), F32),
            VMEM((TOK, WIDE), BF16),
            VMEM((256, WIDE), BF16),
            VMEM((TOK, 256), BF16),
            VMEM((4, 2, 2, TOK, 256), BF16),
            VMEM((4, 2, 2, HALF, TOK), F32),
            VMEM((4, WIDE, WIDE), BF16),
            VMEM((3, 4, 2, 2, HALF, TOK), BF16),
            VMEM((3, 2, 2, 2, HALF, TOK), BF16),
            VMEM((3, 2, 2, HALF, TOK), BF16),
            VMEM((3, 2, 2, HALF, TOK), BF16),
            VMEM((3, 2, HALF, TOK), BF16),
            VMEM((3, 2, HALF, TOK), BF16),
            VMEM((3, COLS, TOK), F32),
            VMEM((4, 2, TOK, 256), BF16),
            VMEM((4, 2, TOK, 256), BF16),
            VMEM((7, TOK, 256), BF16),
            pltpu.SemaphoreType.DMA((8,)),
            pltpu.SemaphoreType.DMA((7,)),
            pltpu.SemaphoreType.DMA((7,)),
            pltpu.SemaphoreType.DMA((8,)),
            pltpu.SemaphoreType.DMA((8,)),
            pltpu.SemaphoreType.DMA((4, 2, 3)),
            pltpu.SemaphoreType.DMA((2, 3, 2, 5)),
            pltpu.SemaphoreType.DMA((2, 8)),
        ],
        compiler_params=pltpu.CompilerParams(
            collective_id=0, has_side_effects=True, vmem_limit_bytes=60 << 20
        ),
        name="attention_back",
    )(
        resp_lengths, resp_prompt, q_prompt, k_prompt, v_prompt, do_prompt,
        q_resp, k_resp, v_resp, do_resp, w_query, w_key, w_value,
    )


def solution(mesh):
    return jax.shard_map(
        shards,
        mesh=mesh,
        in_specs=(P("seq", "head"),) * 8 + (P("seq", None),) * 2 + (P(None, "head"),) * 3,
        out_specs=(P("seq", "head"), P("seq", "head")),
        check_vma=False,
    )
```

```python
import functools
import math

import jax
import jax.numpy as jnp
from jax import lax
from jax.experimental import pallas as pl
from jax.experimental.pallas import tpu as pltpu
from jax.sharding import PartitionSpec as P

MESH = pl.DeviceIdType.MESH
VMEM = pltpu.VMEM
BF16 = jnp.bfloat16
F32 = jnp.float32
HD = 128
GROUP = 8
TOK = 128
NEG = -1e30
SCALE = 1.0 / math.sqrt(HD)
EXP2 = SCALE * math.log2(math.e)
D = 5120
COLS = 640
HALF = 320
WIDE = 1280
NT = (((1,), (1,)), ((), ()))
NN = (((1,), (0,)), ((), ()))


def dot(a, b, dims):
    return lax.dot_general(a, b, dims, preferred_element_type=F32)


def remote(src, dst, send, recv, seq, head):
    return pltpu.make_async_remote_copy(
        src_ref=src, dst_ref=dst, send_sem=send, recv_sem=recv,
        device_id=(seq, head), device_id_type=MESH,
    )


def seq_place():
    n = lax.axis_index("seq")
    return n // 4, lax.rem(n // 2, 2), lax.rem(n, 2)


def seq_peer(dy, dx):
    y, x, c = seq_place()
    return lax.rem(y + dy + 4, 4) * 4 + lax.rem(x + dx, 2) * 2 + c


def seq_sibling():
    n = lax.axis_index("seq")
    return n + 1 - 2 * lax.rem(n, 2)


SEQ_STEPS = [(0, 1), (1, 0), (3, 0), (2, 0), (1, 1), (3, 1), (2, 1)]


def head_peers():
    h = lax.axis_index("head")
    x, z = h // 4, lax.rem(h, 4)
    base = x * 4
    z1 = base + z + 1 - 2 * lax.rem(z, 2)
    z3 = base + 3 - z
    flip = (1 - x) * 4 + z
    return z1, z3, flip


def gather_copies(kv, send, recv, fsend, frecv):
    n, head = lax.axis_index("seq"), lax.axis_index("head")
    copies = [remote(kv.at[n], kv.at[n], fsend.at[0], frecv.at[0], seq_sibling(), head)]
    for j, (dy, dx) in enumerate(SEQ_STEPS[:4]):
        copies.append(remote(kv.at[n], kv.at[n], send.at[j], recv.at[j], seq_peer(dy, dx), head))
    return copies


def gather_start(kv, send, recv, fsend, frecv):
    for copy in gather_copies(kv, send, recv, fsend, frecv):
        copy.start()


def gather_finish(kv, send, recv, fsend, frecv):
    head = lax.axis_index("head")
    sib = seq_sibling()
    copies = gather_copies(kv, send, recv, fsend, frecv)
    partner = seq_peer(0, 1)
    copies[1].wait_recv()
    for j, (dy, _) in enumerate(SEQ_STEPS[4:]):
        passed = remote(
            kv.at[partner], kv.at[partner], send.at[4 + j], recv.at[4 + j], seq_peer(dy, 0), head
        )
        passed.start()
        copies.append(passed)
    forwards = []
    for j, (dy, dx) in enumerate(SEQ_STEPS):
        src = seq_peer(-dy, dx)
        if j > 0:
            copies[j + 1].wait_recv()
        forward = remote(kv.at[src], kv.at[src], fsend.at[j + 1], frecv.at[j + 1], sib, head)
        forward.start()
        forwards.append(forward)
    for copy in [copies[0]] + forwards:
        copy.wait_recv()
    for copy in copies + forwards:
        copy.wait_send()


def segment_of(place, lens_ref):
    end = jnp.int32(0)
    seg = jnp.zeros(place.shape, jnp.int32)
    for c in range(4):
        end = end + lens_ref[0, c]
        seg = seg + (place >= end).astype(jnp.int32)
    return seg


def prompt_of(seg, prompt_ref):
    out = jnp.zeros(seg.shape, jnp.int32)
    for c in range(4):
        out = jnp.where(seg == c, prompt_ref[0, c], out)
    return out


def load_keys(kv, k_r, v_r, kke, vve):
    for r in range(8):
        rows = pl.ds(r * TOK, TOK)
        kke[rows, :HD] = kv[r, 0]
        kke[rows, HD:] = kv[8 + r, 0]
        vve[rows, :HD] = kv[r, 1]
        vve[rows, HD:] = kv[8 + r, 1]
    local = pl.ds(1024, 256)
    kke[local, :HD] = k_r[...]
    kke[local, HD:] = k_r[...]
    vve[local, :HD] = v_r[...]
    vve[local, HD:] = v_r[...]


def turn_keys(kke, kket):
    for r in range(10):
        rows = pl.ds(r * TOK, TOK)
        kket[:, rows] = kke[rows, :].T


def load_rows(q, do, col_prompt, qext, doext):
    first = col_prompt == 0
    zero = jnp.zeros((TOK, HD), BF16)
    first = jnp.broadcast_to(first, (TOK, HD))
    for h in range(GROUP):
        lanes = pl.ds(h * HD, HD)
        rows = pl.ds(h * TOK, TOK)
        qv, dov = q[:, lanes], do[:, lanes]
        qext[rows, :HD] = jnp.where(first, qv, zero)
        qext[rows, HD:] = jnp.where(first, zero, qv)
        doext[rows, :HD] = jnp.where(first, dov, zero)
        doext[rows, HD:] = jnp.where(first, zero, dov)


def fold(x, op):
    return op(x.reshape(x.shape[0] // 8, 8, x.shape[1]), axis=0)


def key_groups(keys):
    size = 256
    return [(k, min(size, keys - k)) for k in range(0, keys, size)]


def chunk_scores(keys, bias_of, qext, doext, kke, vve, s_refs, dp_refs, et, dst):
    low = jnp.full((8, 256), NEG, F32)

    def scores(hp, group, top):
        start, size = group
        s = dot(kke[start : start + size, :], qext[hp * 256 : hp * 256 + 256, :], NT)
        for j in range(0, size, TOK):
            tile = bias_of((start + j) // TOK, s[j : j + TOK])
            s_refs[hp % 2][start + j : start + j + TOK, :] = tile
            top = jnp.maximum(top, fold(tile, jnp.max))
        return top

    def grads(hp, group):
        span = slice(group[0], group[0] + group[1])
        dp_refs[hp % 2][span, :] = dot(vve[span, :], doext[hp * 256 : hp * 256 + 256, :], NT)

    def tiles(group):
        return [slice(j, j + TOK) for j in range(group[0], group[0] + group[1], TOK)]

    groups = key_groups(keys)
    top = low
    for group in groups:
        top = scores(0, group, top)
        grads(0, group)
    for hp in range(4):
        s_ref, dp_ref = s_refs[hp % 2], dp_refs[hp % 2]
        cols = slice(hp * 256, hp * 256 + 256)
        top = jnp.max(top, axis=0, keepdims=True)
        norm = jnp.zeros((8, 256), F32)
        weighted = jnp.zeros((8, 256), F32)
        next_top = low
        for group in groups:
            if hp < 3:
                next_top = scores(hp + 1, group, next_top)
            for span in tiles(group):
                e = jnp.exp2((s_ref[span, :] - top) * EXP2)
                s_ref[span, :] = e
                norm = norm + fold(e, jnp.sum)
                weighted = weighted + fold(e * dp_ref[span, :], jnp.sum)
        inv = 1.0 / jnp.sum(norm, axis=0, keepdims=True)
        mean = jnp.sum(weighted, axis=0, keepdims=True) * inv
        for group in groups:
            if hp < 3:
                grads(hp + 1, group)
            for span in tiles(group):
                p = s_ref[span, :] * inv
                et[span, cols] = p.astype(BF16)
                dst[span, cols] = (p * (dp_ref[span, :] - mean)).astype(BF16)
        top = next_top


def chunk_product(low, high, first, left, right, total):
    for start, size in key_groups(high - low):
        span = slice(low + start, low + start + size)
        value = dot(left[span, :], right[...], NN)
        if first:
            total[span, :] = value
        else:
            total[span, :] += value


def chunk_dq(keys, row_prompt, kket, dst, dq_ref, rows_out):
    first = row_prompt == 0
    for hp in range(4):
        both = dot(kket[:, :keys], dst[:keys, hp * 256 : hp * 256 + 256], NN)
        for k in range(2):
            lanes = slice(k * TOK, (k + 1) * TOK)
            part = jnp.where(first, both[:HD, lanes], both[HD:, lanes]) * SCALE
            h = hp * 2 + k
            dq_ref[rows_out, h * HD : (h + 1) * HD] = part.T.astype(BF16)


SIDES = (
    dict(give=(1, 3), keep=(0, 3), last=1),
    dict(give=(2, 4), keep=(1, 0), last=0),
)


def owner_of(offset, side):
    h = lax.axis_index("head")
    x, z = h // 4, lax.rem(h, 4)
    if offset == 0:
        oz = z
    elif offset == 1:
        oz = z + 1 - 2 * lax.rem(z, 2)
    elif offset == 2:
        oz = lax.rem(z + 2, 4)
    else:
        oz = 3 - z
    ox = x if side == 0 else 1 - x
    return ox * 4 + oz


WEIGHT_ORDER = (2, 1, 3, 0)


def weight_copies(offsets, w_q, w_k, w_v, w, sem):
    for offset in offsets:
        for side in range(2):
            rows = pl.ds(pl.multiple_of(owner_of(offset, side) * COLS, COLS), COLS)
            into = pl.ds(side * COLS, COLS)
            yield from [
                pltpu.make_async_copy(w_q.at[rows], w.at[offset, into, pl.ds(0, 1024)], sem.at[offset, side, 0]),
                pltpu.make_async_copy(w_k.at[rows], w.at[offset, into, pl.ds(1024, HD)], sem.at[offset, side, 1]),
                pltpu.make_async_copy(w_v.at[rows], w.at[offset, into, pl.ds(1152, HD)], sem.at[offset, side, 2]),
            ]


class HeadSum:
    def __init__(self, chunk, pieces, terms, r1, s2, r2, s3, r3, sums, sems):
        self.chunk = chunk
        self.size = HALF // pieces
        self.parts = [(half, piece) for piece in range(pieces) for half in range(2)]
        self.terms, self.r1, self.s2, self.r2, self.s3, self.r3 = (
            terms.at[chunk], r1.at[chunk], s2.at[chunk], r2.at[chunk], s3.at[chunk], r3.at[chunk]
        )
        self.sums = sums.at[chunk]
        self.sems = sems
        self.seq = lax.axis_index("seq")
        self.z1, self.z3, self.flip = head_peers()

    def rows(self, part):
        return pl.ds(part[1] * self.size, self.size)

    def copy(self, part, step):
        half, piece = part
        rows = self.rows(part)
        send, recv = (self.sems.at[k, self.chunk, half, step, piece] for k in range(2))
        near, far = (self.z1, self.z3) if half == 0 else (self.z3, self.z1)
        if step < 2:
            side = 1 - step
            low, high = SIDES[half]["give"]
            src = self.terms.at[pl.ds(low, high - low), half, side, rows]
            return remote(src, self.r1.at[half, side, :, rows], send, recv, self.seq, near)
        if step < 4:
            k = step - 2
            return remote(
                self.s2.at[half, k, rows], self.r2.at[half, k, rows], send, recv, self.seq, self.flip
            )
        return remote(self.s3.at[half, rows], self.r3.at[half, rows], send, recv, self.seq, far)

    def first(self, half):
        for step in range(2):
            for part in self.parts:
                if part[0] == half:
                    self.copy(part, step).start()

    def cross(self, part, k):
        half, rows = part[0], self.rows(part)
        offset = SIDES[half]["keep"][k]
        total = self.terms[offset, half, 1, rows].astype(F32) + self.r1[half, 1, k, rows].astype(F32)
        self.s2[half, k, rows] = total.astype(BF16)
        self.copy(part, 2 + k).start()

    def second(self):
        for part in self.parts:
            self.copy(part, 0).wait_recv()
            self.cross(part, SIDES[part[0]]["last"])
        for part in self.parts:
            self.cross(part, 1 - SIDES[part[0]]["last"])

    def kept(self, part, k):
        half, rows = part[0], self.rows(part)
        self.copy(part, 2 + k).wait_recv()
        offset = SIDES[half]["keep"][k]
        return (
            self.terms[offset, half, 0, rows].astype(F32)
            + self.r1[half, 0, k, rows].astype(F32)
            + self.r2[half, k, rows].astype(F32)
        )

    def third(self):
        for part in self.parts:
            self.copy(part, 1).wait_recv()
            total = self.kept(part, SIDES[part[0]]["last"])
            self.s3[part[0], self.rows(part)] = total.astype(BF16)
            self.copy(part, 4).start()

    def final(self):
        for part in self.parts:
            total = self.kept(part, 1 - SIDES[part[0]]["last"])
            self.copy(part, 4).wait_recv()
            start = part[0] * HALF + part[1] * self.size
            self.sums[start : start + self.size, :] = total + self.r3[
                part[0], self.rows(part)
            ].astype(F32)

    def write(self, out, base):
        for part in range(5):
            lanes = slice(part * TOK, (part + 1) * TOK)
            out[base : base + TOK, lanes] = self.sums[lanes, :].T.astype(BF16)

    def drain(self):
        for part in self.parts:
            for step in range(5):
                self.copy(part, step).wait_send()


BLOCKS = ((1, 0), (1, 1), (0, 0), (0, 1))


def block_rows(side, half):
    start = side * COLS + half * HALF
    return slice(start, start + HALF)


def grads_sibling(group, grads, rc, gsem):
    c = lax.rem(lax.axis_index("seq"), 2)
    return remote(
        grads.at[group, 1 - c], rc.at[group], gsem.at[0, 7 + group], gsem.at[1, 7 + group],
        seq_sibling(), lax.axis_index("head"),
    )


def grads_copies(gs, rg, gsem):
    y, x, c = seq_place()
    copies = []
    for j, (dy, dx) in enumerate(SEQ_STEPS):
        oy = lax.rem(y + dy, 4)
        ox = lax.rem(x + dx, 2)
        block = lax.rem(oy, 2) * 2 + ox
        copies.append(
            remote(
                gs.at[block, oy // 2], rg.at[j], gsem.at[0, j], gsem.at[1, j],
                seq_peer(dy, dx), lax.axis_index("head"),
            )
        )
    return copies


def grads_second(grads, rc, gs, rg, gsem):
    c = lax.rem(lax.axis_index("seq"), 2)
    for b in range(4):
        grads_sibling(b, grads, rc, gsem).wait_recv()
        for p in range(2):
            gs[b, p] = (grads[b, c, p].astype(F32) + rc[b, p].astype(F32)).astype(BF16)
    for copy in grads_copies(gs, rg, gsem):
        copy.start()


def grads_finish(gs, rg, gsem, d_p):
    y, x, c = seq_place()
    total = gs[lax.rem(y, 2) * 2 + x, y // 2].astype(F32)
    for j, copy in enumerate(grads_copies(gs, rg, gsem)):
        copy.wait_recv()
        total = total + rg[j].astype(F32)
    d_p[...] = total.astype(BF16)


def whole_kernel(
    lens_ref, prompt_ref, q_p_h, k_p_h, v_p_h, do_p_h, q_r_h, k_r_h, v_r_h, do_r_h, w_q, w_k, w_v,
    out,
    kv, q_p, do_p, q_r, do_r, k_r, v_r,
    kke, vve, kket, qext, doext, s0, s1, dp0, dp1, et, dst, dkk, dvv, bias0, bias1, d_b, d_ap, late, grads, early,
    w, terms, r1, s2, r2, s3, r3, totals, rc, gs, rg,
    lsem, send, recv, fsend, frecv, wsem, hsem, gsem,
):
    seq, head = lax.axis_index("seq"), lax.axis_index("head")
    barrier = pltpu.get_barrier_semaphore()
    seqs = [seq_sibling()] + [seq_peer(dy, dx) for dy, dx in SEQ_STEPS]
    heads = list(head_peers())
    for peer in seqs:
        pl.semaphore_signal(barrier, inc=1, device_id=(peer, head), device_id_type=MESH)
    for peer in heads:
        pl.semaphore_signal(barrier, inc=1, device_id=(seq, peer), device_id_type=MESH)
    loads = [
        pltpu.make_async_copy(src, dst_ref, lsem.at[k])
        for k, (src, dst_ref) in enumerate((
            (k_p_h, kv.at[seq, 0]), (v_p_h, kv.at[seq, 1]), (q_r_h, q_r), (do_r_h, do_r),
            (k_r_h, k_r), (v_r_h, v_r), (q_p_h, q_p), (do_p_h, do_p),
        ))
    ]
    for copy in loads:
        copy.start()
    for copy in loads[:2]:
        copy.wait()
    pl.semaphore_wait(barrier, len(seqs) + len(heads))
    gather_start(kv, send, recv, fsend, frecv)
    for copy in weight_copies(WEIGHT_ORDER, w_q, w_k, w_v, w, wsem):
        copy.start()
    for copy in loads[2:]:
        copy.wait()
    sums = [HeadSum(c, (1, 1, 2)[c], terms, r1, s2, r2, s3, r3, totals, hsem) for c in range(3)]
    mine = seq // 8

    row_prompts = []
    for half, bias in ((0, bias0), (1, bias1)):
        base = half * TOK
        col = base + lax.broadcasted_iota(jnp.int32, (TOK, 1), 0)
        row = base + lax.rem(lax.broadcasted_iota(jnp.int32, (1, 256), 1), TOK)
        row_seg = segment_of(row, lens_ref)
        row_prompts.append(prompt_of(row_seg[:, :TOK], prompt_ref))
        key = lax.broadcasted_iota(jnp.int32, (base + TOK, 1), 0)
        key_seg = segment_of(key, lens_ref)
        seen = (key_seg == row_seg) & (key <= row)
        bias[...] = jnp.where(seen, 0.0, NEG)
        span = slice(base, base + TOK)
        load_rows(
            q_r.at[span], do_r.at[span], prompt_of(segment_of(col, lens_ref), prompt_ref),
            qext.at[half], doext.at[half],
        )
    load_rows(q_p, do_p, jnp.full((TOK, 1), mine, jnp.int32), qext.at[2], doext.at[2])
    diff = (
        lax.rem(seq, 8) * TOK
        + lax.rem(lax.broadcasted_iota(jnp.int32, (TOK, 256), 1), TOK)
        - lax.broadcasted_iota(jnp.int32, (TOK, 256), 0)
    )
    d_ap[TOK:, 1024:] = jnp.zeros((TOK, 256), BF16)
    gather_finish(kv, send, recv, fsend, frecv)
    load_keys(kv, k_r, v_r, kke, vve)

    def scores(keys, bias_of, chunk):
        chunk_scores(
            keys, bias_of, qext.at[chunk], doext.at[chunk], kke, vve, (s0, s1), (dp0, dp1), et, dst
        )

    def response(half, first):
        bias = (bias0, bias1)[half]
        keys = 1024 + (half + 1) * TOK

        def local_bias(t, s):
            if t < 8:
                return s
            return s + bias[(t - 8) * TOK : (t - 7) * TOK, :]

        scores(keys, local_bias, half)
        if first:
            turn_keys(kke, kket)
        chunk_product(0, keys, first, et, doext.at[half], dvv)
        chunk_product(0, keys, first, dst, qext.at[half], dkk)
        rows = (d_ap, d_b)[half]
        chunk_dq(keys, row_prompts[half], kket, dst, rows, slice(0, TOK))
        local = slice(1024 + half * TOK, 1024 + half * TOK + TOK)
        rows[:TOK, 1024:1152] = ((dkk[local, :HD] + dkk[local, HD:]) * SCALE).astype(BF16)
        rows[:TOK, 1152:] = (dvv[local, :HD] + dvv[local, HD:]).astype(BF16)

    def wait_weights(offset):
        for copy in weight_copies((offset,), w_q, w_k, w_v, w, wsem):
            copy.wait()

    def start(chunk, offset):
        if offset in (1, 3):
            sums[chunk].first(offset // 2)

    response(1, True)
    for offset in WEIGHT_ORDER:
        wait_weights(offset)
        for side, half in BLOCKS:
            value = dot(w[offset, block_rows(side, half), :], d_b[...], NT)
            terms[1, offset, half, side] = value.astype(BF16)
        start(1, offset)
    response(0, False)
    sums[1].second()

    scores(1024, lambda t, s: jnp.where(diff >= t * TOK, s, NEG), 2)
    for g in range(4):
        chunk_product(g * 256, g * 256 + 256, False, et, doext.at[2], dvv)
        chunk_product(g * 256, g * 256 + 256, False, dst, qext.at[2], dkk)
        for r in range(2):
            keys = slice(g * 256 + r * TOK, g * 256 + r * TOK + TOK)
            for p in range(2):
                lanes = slice(p * HD, (p + 1) * HD)
                grads[g, r, p, :, :HD] = (dkk[keys, lanes] * SCALE).astype(BF16)
                grads[g, r, p, :, HD:] = dvv[keys, lanes].astype(BF16)
        grads_sibling(g, grads, rc, gsem).start()
    chunk_dq(1024, jnp.full((1, TOK), mine, jnp.int32), kket, dst, d_ap, slice(TOK, 256))
    sums[1].third()
    grads_second(grads, rc, gs, rg, gsem)
    for offset in WEIGHT_ORDER:
        for side, half in BLOCKS:
            value = dot(w[offset, block_rows(side, half), :], d_ap[...], NT)
            terms[0, offset, half, side] = value[:, :TOK].astype(BF16)
            early[offset, half, side] = value[:, TOK:]
        start(0, offset)
    sums[1].final()
    sums[1].write(out, 2 * TOK)
    sums[0].second()
    grads_finish(gs, rg, gsem, late)
    for offset in WEIGHT_ORDER:
        for side, half in BLOCKS:
            value = dot(w[offset, block_rows(side, half), 1024:], late[...], NT)
            terms[2, offset, half, side] = (early[offset, half, side] + value).astype(BF16)
        start(2, offset)
    sums[0].third()
    sums[2].second()
    sums[0].final()
    sums[0].write(out, TOK)
    sums[2].third()
    sums[2].final()
    sums[2].write(out, 0)
    for g in range(4):
        grads_sibling(g, grads, rc, gsem).wait_send()
    for copy in grads_copies(gs, rg, gsem):
        copy.wait_send()
    for c in range(3):
        sums[c].drain()


def split_kernel(both, out_p, out_r):
    out_p[...] = both[:TOK, :]
    out_r[...] = both[TOK:, :]


def shards(
    q_prompt, k_prompt, v_prompt, do_prompt, q_resp, k_resp, v_resp, do_resp,
    resp_lengths, resp_prompt, w_query, w_key, w_value,
):
    whole = pl.BlockSpec(memory_space=VMEM)
    hbm = pl.BlockSpec(memory_space=pl.ANY)
    scalars = pl.BlockSpec(memory_space=pltpu.SMEM)
    both = pl.pallas_call(
        whole_kernel,
        out_shape=jax.ShapeDtypeStruct((3 * TOK, COLS), BF16),
        in_specs=[scalars] * 2 + [hbm] * 11,
        out_specs=whole,
        scratch_shapes=[
            VMEM((16, 2, TOK, HD), BF16),
            VMEM((TOK, 1024), BF16),
            VMEM((TOK, 1024), BF16),
            VMEM((256, 1024), BF16),
            VMEM((256, 1024), BF16),
            VMEM((256, HD), BF16),
            VMEM((256, HD), BF16),
            VMEM((WIDE, 256), BF16),
            VMEM((WIDE, 256), BF16),
            VMEM((256, WIDE), BF16),
            VMEM((3, 1024, 256), BF16),
            VMEM((3, 1024, 256), BF16),
            VMEM((WIDE, 256), F32),
            VMEM((WIDE, 256), F32),
            VMEM((WIDE, 256), F32),
            VMEM((WIDE, 256), F32),
            VMEM((WIDE, 1024), BF16),
            VMEM((WIDE, 1024), BF16),
            VMEM((WIDE, 256), F32),
            VMEM((WIDE, 256), F32),
            VMEM((TOK, 256), F32),
            VMEM((256, 256), F32),
            VMEM((TOK, WIDE), BF16),
            VMEM((256, WIDE), BF16),
            VMEM((TOK, 256), BF16),
            VMEM((4, 2, 2, TOK, 256), BF16),
            VMEM((4, 2, 2, HALF, TOK), F32),
            VMEM((4, WIDE, WIDE), BF16),
            VMEM((3, 4, 2, 2, HALF, TOK), BF16),
            VMEM((3, 2, 2, 2, HALF, TOK), BF16),
            VMEM((3, 2, 2, HALF, TOK), BF16),
            VMEM((3, 2, 2, HALF, TOK), BF16),
            VMEM((3, 2, HALF, TOK), BF16),
            VMEM((3, 2, HALF, TOK), BF16),
            VMEM((3, COLS, TOK), F32),
            VMEM((4, 2, TOK, 256), BF16),
            VMEM((4, 2, TOK, 256), BF16),
            VMEM((7, TOK, 256), BF16),
            pltpu.SemaphoreType.DMA((8,)),
            pltpu.SemaphoreType.DMA((7,)),
            pltpu.SemaphoreType.DMA((7,)),
            pltpu.SemaphoreType.DMA((8,)),
            pltpu.SemaphoreType.DMA((8,)),
            pltpu.SemaphoreType.DMA((4, 2, 3)),
            pltpu.SemaphoreType.DMA((2, 3, 2, 5, 2)),
            pltpu.SemaphoreType.DMA((2, 11)),
        ],
        compiler_params=pltpu.CompilerParams(
            collective_id=0, has_side_effects=True, vmem_limit_bytes=60 << 20
        ),
        name="attention_back",
    )(
        resp_lengths, resp_prompt, q_prompt, k_prompt, v_prompt, do_prompt,
        q_resp, k_resp, v_resp, do_resp, w_query, w_key, w_value,
    )
    return pl.pallas_call(
        split_kernel,
        out_shape=(
            jax.ShapeDtypeStruct((TOK, COLS), BF16),
            jax.ShapeDtypeStruct((2 * TOK, COLS), BF16),
        ),
        in_specs=[whole],
        out_specs=(whole, whole),
        name="split_rows",
    )(both)


def solution(mesh):
    return jax.shard_map(
        shards,
        mesh=mesh,
        in_specs=(P("seq", "head"),) * 8 + (P("seq", None),) * 2 + (P(None, "head"),) * 3,
        out_specs=(P("seq", "head"), P("seq", "head")),
        check_vma=False,
    )
```

```python
import functools
import math

import jax
import jax.numpy as jnp
from jax import lax
from jax.experimental import pallas as pl
from jax.experimental.pallas import tpu as pltpu
from jax.sharding import PartitionSpec as P

MESH = pl.DeviceIdType.MESH
VMEM = pltpu.VMEM
BF16 = jnp.bfloat16
F32 = jnp.float32
HD = 128
GROUP = 8
TOK = 128
NEG = -1e30
SCALE = 1.0 / math.sqrt(HD)
EXP2 = SCALE * math.log2(math.e)
D = 5120
COLS = 640
HALF = 320
WIDE = 1280
NT = (((1,), (1,)), ((), ()))
NN = (((1,), (0,)), ((), ()))


def dot(a, b, dims):
    return lax.dot_general(a, b, dims, preferred_element_type=F32)


def remote(src, dst, send, recv, seq, head):
    return pltpu.make_async_remote_copy(
        src_ref=src, dst_ref=dst, send_sem=send, recv_sem=recv,
        device_id=(seq, head), device_id_type=MESH,
    )


def seq_place():
    n = lax.axis_index("seq")
    return n // 4, lax.rem(n // 2, 2), lax.rem(n, 2)


def seq_peer(dy, dx):
    y, x, c = seq_place()
    return lax.rem(y + dy + 4, 4) * 4 + lax.rem(x + dx, 2) * 2 + c


def seq_sibling():
    n = lax.axis_index("seq")
    return n + 1 - 2 * lax.rem(n, 2)


SEQ_STEPS = [(0, 1), (1, 0), (3, 0), (2, 0), (1, 1), (3, 1), (2, 1)]


def head_peers():
    h = lax.axis_index("head")
    x, z = h // 4, lax.rem(h, 4)
    base = x * 4
    z1 = base + z + 1 - 2 * lax.rem(z, 2)
    z3 = base + 3 - z
    flip = (1 - x) * 4 + z
    return z1, z3, flip


def key_block(ref, n):
    rows = pl.ds(pl.multiple_of(lax.rem(n, 8) * TOK, TOK), TOK)
    lanes = pl.ds(pl.multiple_of(n // 8 * HD, HD), HD)
    return ref.at[rows, lanes]


def block_pair(keys, n, send, recv, slot, seq):
    head = lax.axis_index("head")
    return [
        remote(key_block(ref, n), key_block(ref, n), send.at[slot, k], recv.at[slot, k], seq, head)
        for k, ref in enumerate(keys)
    ]


def gather_pairs(keys, send, recv, fsend, frecv):
    n = lax.axis_index("seq")
    pairs = []
    for j, (dy, dx) in enumerate(SEQ_STEPS[:4]):
        pairs.append(block_pair(keys, n, send, recv, j, seq_peer(dy, dx)))
    return pairs, block_pair(keys, n, fsend, frecv, 0, seq_sibling())


def gather_start(keys, send, recv, fsend, frecv):
    pairs, own = gather_pairs(keys, send, recv, fsend, frecv)
    for pair in pairs:
        for copy in pair:
            copy.start()
    for copy in own:
        copy.start()


def gather_finish(keys, send, recv, fsend, frecv):
    pairs, own = gather_pairs(keys, send, recv, fsend, frecv)
    partner = seq_peer(0, 1)
    for j, (dy, _) in enumerate(SEQ_STEPS[4:]):
        pairs.append(block_pair(keys, partner, send, recv, 4 + j, seq_peer(dy, 0)))
    forwards = [
        block_pair(keys, seq_peer(-dy, dx), fsend, frecv, j + 1, seq_sibling())
        for j, (dy, dx) in enumerate(SEQ_STEPS)
    ]
    for k in range(2):
        pairs[0][k].wait_recv()
        for pair in pairs[4:]:
            pair[k].start()
    for j in range(7):
        for k in range(2):
            if j > 0:
                pairs[j][k].wait_recv()
            forwards[j][k].start()
    for pair in [own] + forwards:
        for copy in pair:
            copy.wait_recv()
    for pair in pairs + [own] + forwards:
        for copy in pair:
            copy.wait_send()


def segment_of(place, lens_ref):
    end = jnp.int32(0)
    seg = jnp.zeros(place.shape, jnp.int32)
    for c in range(4):
        end = end + lens_ref[0, c]
        seg = seg + (place >= end).astype(jnp.int32)
    return seg


def prompt_of(seg, prompt_ref):
    out = jnp.zeros(seg.shape, jnp.int32)
    for c in range(4):
        out = jnp.where(seg == c, prompt_ref[0, c], out)
    return out


def load_keys(k_r, v_r, kke, vve):
    local = pl.ds(1024, 256)
    kke[local, :HD] = k_r[...]
    kke[local, HD:] = k_r[...]
    vve[local, :HD] = v_r[...]
    vve[local, HD:] = v_r[...]


def turn_keys(kke, kket):
    for r in range(10):
        rows = pl.ds(r * TOK, TOK)
        kket[:, rows] = kke[rows, :].T


def load_rows(q, do, col_prompt, qext, doext):
    first = col_prompt == 0
    zero = jnp.zeros((TOK, HD), BF16)
    first = jnp.broadcast_to(first, (TOK, HD))
    for h in range(GROUP):
        lanes = pl.ds(h * HD, HD)
        rows = pl.ds(h * TOK, TOK)
        qv, dov = q[:, lanes], do[:, lanes]
        qext[rows, :HD] = jnp.where(first, qv, zero)
        qext[rows, HD:] = jnp.where(first, zero, qv)
        doext[rows, :HD] = jnp.where(first, dov, zero)
        doext[rows, HD:] = jnp.where(first, zero, dov)


def fold(x, op):
    return op(x.reshape(x.shape[0] // 8, 8, x.shape[1]), axis=0)


def key_groups(keys):
    size = 256
    return [(k, min(size, keys - k)) for k in range(0, keys, size)]


def chunk_scores(keys, bias_of, qext, doext, kke, vve, s_refs, dp_refs, et, dst):
    low = jnp.full((8, 256), NEG, F32)

    def scores(hp, group, top):
        start, size = group
        s = dot(kke[start : start + size, :], qext[hp * 256 : hp * 256 + 256, :], NT)
        for j in range(0, size, TOK):
            tile = bias_of((start + j) // TOK, s[j : j + TOK])
            s_refs[hp % 2][start + j : start + j + TOK, :] = tile
            top = jnp.maximum(top, fold(tile, jnp.max))
        return top

    def grads(hp, group):
        span = slice(group[0], group[0] + group[1])
        dp_refs[hp % 2][span, :] = dot(vve[span, :], doext[hp * 256 : hp * 256 + 256, :], NT)

    def tiles(group):
        return [slice(j, j + TOK) for j in range(group[0], group[0] + group[1], TOK)]

    groups = key_groups(keys)
    top = low
    for group in groups:
        top = scores(0, group, top)
        grads(0, group)
    for hp in range(4):
        s_ref, dp_ref = s_refs[hp % 2], dp_refs[hp % 2]
        cols = slice(hp * 256, hp * 256 + 256)
        top = jnp.max(top, axis=0, keepdims=True)
        norm = jnp.zeros((8, 256), F32)
        weighted = jnp.zeros((8, 256), F32)
        next_top = low
        for group in groups:
            if hp < 3:
                next_top = scores(hp + 1, group, next_top)
            for span in tiles(group):
                e = jnp.exp2((s_ref[span, :] - top) * EXP2)
                s_ref[span, :] = e
                norm = norm + fold(e, jnp.sum)
                weighted = weighted + fold(e * dp_ref[span, :], jnp.sum)
        inv = 1.0 / jnp.sum(norm, axis=0, keepdims=True)
        mean = jnp.sum(weighted, axis=0, keepdims=True) * inv
        for group in groups:
            if hp < 3:
                grads(hp + 1, group)
            for span in tiles(group):
                p = s_ref[span, :] * inv
                et[span, cols] = p.astype(BF16)
                dst[span, cols] = (p * (dp_ref[span, :] - mean)).astype(BF16)
        top = next_top


def chunk_product(low, high, first, left, right, total):
    for start, size in key_groups(high - low):
        span = slice(low + start, low + start + size)
        value = dot(left[span, :], right[...], NN)
        if first:
            total[span, :] = value
        else:
            total[span, :] += value


def chunk_dq(keys, row_prompt, kket, dst, dq_ref, rows_out):
    first = row_prompt == 0
    for hp in range(4):
        both = dot(kket[:, :keys], dst[:keys, hp * 256 : hp * 256 + 256], NN)
        for k in range(2):
            lanes = slice(k * TOK, (k + 1) * TOK)
            part = jnp.where(first, both[:HD, lanes], both[HD:, lanes]) * SCALE
            h = hp * 2 + k
            dq_ref[rows_out, h * HD : (h + 1) * HD] = part.T.astype(BF16)


SIDES = (
    dict(give=(1, 3), keep=(0, 3), last=1),
    dict(give=(2, 4), keep=(1, 0), last=0),
)


def owner_of(offset, side):
    h = lax.axis_index("head")
    x, z = h // 4, lax.rem(h, 4)
    if offset == 0:
        oz = z
    elif offset == 1:
        oz = z + 1 - 2 * lax.rem(z, 2)
    elif offset == 2:
        oz = lax.rem(z + 2, 4)
    else:
        oz = 3 - z
    ox = x if side == 0 else 1 - x
    return ox * 4 + oz


WEIGHT_ORDER = (2, 1, 3, 0)


def weight_copies(offsets, w_q, w_k, w_v, w, sem):
    for offset in offsets:
        for side in range(2):
            rows = pl.ds(pl.multiple_of(owner_of(offset, side) * COLS, COLS), COLS)
            into = pl.ds(side * COLS, COLS)
            yield from [
                pltpu.make_async_copy(w_q.at[rows], w.at[offset, into, pl.ds(0, 1024)], sem.at[offset, side, 0]),
                pltpu.make_async_copy(w_k.at[rows], w.at[offset, into, pl.ds(1024, HD)], sem.at[offset, side, 1]),
                pltpu.make_async_copy(w_v.at[rows], w.at[offset, into, pl.ds(1152, HD)], sem.at[offset, side, 2]),
            ]


class HeadSum:
    def __init__(self, chunk, pieces, terms, r1, s2, r2, s3, r3, sums, sems):
        self.chunk = chunk
        self.size = HALF // pieces
        self.parts = [(half, piece) for piece in range(pieces) for half in range(2)]
        self.terms, self.r1, self.s2, self.r2, self.s3, self.r3 = (
            terms.at[chunk], r1.at[chunk], s2.at[chunk], r2.at[chunk], s3.at[chunk], r3.at[chunk]
        )
        self.sums = sums.at[chunk]
        self.sems = sems
        self.seq = lax.axis_index("seq")
        self.z1, self.z3, self.flip = head_peers()

    def rows(self, part):
        return pl.ds(part[1] * self.size, self.size)

    def copy(self, part, step):
        half, piece = part
        rows = self.rows(part)
        send, recv = (self.sems.at[k, self.chunk, half, step, piece] for k in range(2))
        near, far = (self.z1, self.z3) if half == 0 else (self.z3, self.z1)
        if step < 2:
            side = 1 - step
            low, high = SIDES[half]["give"]
            src = self.terms.at[pl.ds(low, high - low), half, side, rows]
            return remote(src, self.r1.at[half, side, :, rows], send, recv, self.seq, near)
        if step < 4:
            k = step - 2
            return remote(
                self.s2.at[half, k, rows], self.r2.at[half, k, rows], send, recv, self.seq, self.flip
            )
        return remote(self.s3.at[half, rows], self.r3.at[half, rows], send, recv, self.seq, far)

    def first(self, half, side):
        for part in self.parts:
            if part[0] == half:
                self.copy(part, 1 - side).start()

    def cross(self, part, k):
        half, rows = part[0], self.rows(part)
        offset = SIDES[half]["keep"][k]
        total = self.terms[offset, half, 1, rows].astype(F32) + self.r1[half, 1, k, rows].astype(F32)
        self.s2[half, k, rows] = total.astype(BF16)
        self.copy(part, 2 + k).start()

    def second(self):
        for part in self.parts:
            self.copy(part, 0).wait_recv()
            self.cross(part, SIDES[part[0]]["last"])
        for part in self.parts:
            self.cross(part, 1 - SIDES[part[0]]["last"])

    def kept(self, part, k):
        half, rows = part[0], self.rows(part)
        self.copy(part, 2 + k).wait_recv()
        offset = SIDES[half]["keep"][k]
        return (
            self.terms[offset, half, 0, rows].astype(F32)
            + self.r1[half, 0, k, rows].astype(F32)
            + self.r2[half, k, rows].astype(F32)
        )

    def third(self):
        for part in self.parts:
            self.copy(part, 1).wait_recv()
            total = self.kept(part, SIDES[part[0]]["last"])
            self.s3[part[0], self.rows(part)] = total.astype(BF16)
            self.copy(part, 4).start()

    def final(self):
        for part in self.parts:
            total = self.kept(part, 1 - SIDES[part[0]]["last"])
            self.copy(part, 4).wait_recv()
            start = part[0] * HALF + part[1] * self.size
            self.sums[start : start + self.size, :] = total + self.r3[
                part[0], self.rows(part)
            ].astype(F32)

    def write(self, out, base):
        for part in range(5):
            lanes = slice(part * TOK, (part + 1) * TOK)
            out[base : base + TOK, lanes] = self.sums[lanes, :].T.astype(BF16)

    def drain(self):
        for part in self.parts:
            for step in range(5):
                self.copy(part, step).wait_send()


GIVEN = (
    ((2, 1, 0), (1, 1, 0)), ((2, 1, 1), (3, 1, 1)), ((2, 0, 0), (1, 0, 0)), ((2, 0, 1), (3, 0, 1)),
)
KEPT = (
    (3, 1, 0), (0, 1, 0), (1, 1, 1), (0, 1, 1), (3, 0, 0), (0, 0, 0), (1, 0, 1), (0, 0, 1),
)


def block_rows(side, half):
    start = side * COLS + half * HALF
    return slice(start, start + HALF)


def grads_sibling(group, grads, rc, gsem):
    c = lax.rem(lax.axis_index("seq"), 2)
    return remote(
        grads.at[group, 1 - c], rc.at[group], gsem.at[0, 7 + group], gsem.at[1, 7 + group],
        seq_sibling(), lax.axis_index("head"),
    )


def grads_copies(gs, rg, gsem):
    y, x, c = seq_place()
    copies = []
    for j, (dy, dx) in enumerate(SEQ_STEPS):
        oy = lax.rem(y + dy, 4)
        ox = lax.rem(x + dx, 2)
        block = lax.rem(oy, 2) * 2 + ox
        copies.append(
            remote(
                gs.at[block, oy // 2], rg.at[j], gsem.at[0, j], gsem.at[1, j],
                seq_peer(dy, dx), lax.axis_index("head"),
            )
        )
    return copies


def grads_second(grads, rc, gs, rg, gsem):
    c = lax.rem(lax.axis_index("seq"), 2)
    for b in range(4):
        grads_sibling(b, grads, rc, gsem).wait_recv()
        for p in range(2):
            gs[b, p] = (grads[b, c, p].astype(F32) + rc[b, p].astype(F32)).astype(BF16)
    for copy in grads_copies(gs, rg, gsem):
        copy.start()


def grads_finish(gs, rg, gsem, d_p):
    y, x, c = seq_place()
    total = gs[lax.rem(y, 2) * 2 + x, y // 2].astype(F32)
    for j, copy in enumerate(grads_copies(gs, rg, gsem)):
        copy.wait_recv()
        total = total + rg[j].astype(F32)
    d_p[...] = total.astype(BF16)


def whole_kernel(
    lens_ref, prompt_ref, q_p_h, k_p_h, v_p_h, do_p_h, q_r_h, k_r_h, v_r_h, do_r_h, w_q, w_k, w_v,
    out,
    q_p, do_p, q_r, do_r, k_r, v_r,
    kke, vve, kket, qext, doext, s0, s1, dp0, dp1, et, dst, dkk, dvv, bias0, bias1, d_b, d_ap, late, grads, early,
    w, terms, r1, s2, r2, s3, r3, totals, rc, gs, rg,
    lsem, send, recv, fsend, frecv, wsem, hsem, gsem,
):
    seq, head = lax.axis_index("seq"), lax.axis_index("head")
    barrier = pltpu.get_barrier_semaphore()
    seqs = [seq_sibling()] + [seq_peer(dy, dx) for dy, dx in SEQ_STEPS]
    heads = list(head_peers())
    for peer in seqs:
        pl.semaphore_signal(barrier, inc=1, device_id=(peer, head), device_id_type=MESH)
    for peer in heads:
        pl.semaphore_signal(barrier, inc=1, device_id=(seq, peer), device_id_type=MESH)
    loads = [
        pltpu.make_async_copy(src, dst_ref, lsem.at[k])
        for k, (src, dst_ref) in enumerate((
            (k_p_h, key_block(kke, seq)), (v_p_h, key_block(vve, seq)), (q_r_h, q_r), (do_r_h, do_r),
            (k_r_h, k_r), (v_r_h, v_r), (q_p_h, q_p), (do_p_h, do_p),
        ))
    ]
    for copy in loads:
        copy.start()
    for copy in loads[:2]:
        copy.wait()
    pl.semaphore_wait(barrier, len(seqs) + len(heads))
    gather_start((kke, vve), send, recv, fsend, frecv)
    for copy in weight_copies(WEIGHT_ORDER, w_q, w_k, w_v, w, wsem):
        copy.start()
    for copy in loads[2:]:
        copy.wait()
    sums = [HeadSum(c, (1, 1, 2)[c], terms, r1, s2, r2, s3, r3, totals, hsem) for c in range(3)]
    mine = seq // 8

    row_prompts = []
    for half, bias in ((0, bias0), (1, bias1)):
        base = half * TOK
        col = base + lax.broadcasted_iota(jnp.int32, (TOK, 1), 0)
        row = base + lax.rem(lax.broadcasted_iota(jnp.int32, (1, 256), 1), TOK)
        row_seg = segment_of(row, lens_ref)
        row_prompts.append(prompt_of(row_seg[:, :TOK], prompt_ref))
        key = lax.broadcasted_iota(jnp.int32, (base + TOK, 1), 0)
        key_seg = segment_of(key, lens_ref)
        seen = (key_seg == row_seg) & (key <= row)
        bias[...] = jnp.where(seen, 0.0, NEG)
        span = slice(base, base + TOK)
        load_rows(
            q_r.at[span], do_r.at[span], prompt_of(segment_of(col, lens_ref), prompt_ref),
            qext.at[half], doext.at[half],
        )
    load_rows(q_p, do_p, jnp.full((TOK, 1), mine, jnp.int32), qext.at[2], doext.at[2])
    diff = (
        lax.rem(seq, 8) * TOK
        + lax.rem(lax.broadcasted_iota(jnp.int32, (TOK, 256), 1), TOK)
        - lax.broadcasted_iota(jnp.int32, (TOK, 256), 0)
    )
    d_ap[TOK:, 1024:] = jnp.zeros((TOK, 256), BF16)
    load_keys(k_r, v_r, kke, vve)
    gather_finish((kke, vve), send, recv, fsend, frecv)

    def scores(keys, bias_of, chunk):
        chunk_scores(
            keys, bias_of, qext.at[chunk], doext.at[chunk], kke, vve, (s0, s1), (dp0, dp1), et, dst
        )

    def response(half, first):
        bias = (bias0, bias1)[half]
        keys = 1024 + (half + 1) * TOK

        def local_bias(t, s):
            if t < 8:
                return s
            return s + bias[(t - 8) * TOK : (t - 7) * TOK, :]

        scores(keys, local_bias, half)
        if first:
            turn_keys(kke, kket)
        chunk_product(0, keys, first, et, doext.at[half], dvv)
        chunk_product(0, keys, first, dst, qext.at[half], dkk)
        if not first:
            sums[1].second()
        rows = (d_ap, d_b)[half]
        chunk_dq(keys, row_prompts[half], kket, dst, rows, slice(0, TOK))
        local = slice(1024 + half * TOK, 1024 + half * TOK + TOK)
        rows[:TOK, 1024:1152] = ((dkk[local, :HD] + dkk[local, HD:]) * SCALE).astype(BF16)
        rows[:TOK, 1152:] = (dvv[local, :HD] + dvv[local, HD:]).astype(BF16)

    def wait_weights(offset):
        for copy in weight_copies((offset,), w_q, w_k, w_v, w, wsem):
            copy.wait()

    def product(block, rows, low=0, high=WIDE):
        offset, side, half = block
        return dot(w[offset, block_rows(side, half), low:high], rows, NT)

    def put(chunk, block, value):
        offset, side, half = block
        terms[chunk, offset, half, side] = value.astype(BF16)

    def give(chunk, value_of):
        for pair in GIVEN:
            for block in pair:
                put(chunk, block, value_of(block))
            sums[chunk].first(pair[0][2], pair[0][1])

    response(1, True)
    for offset in WEIGHT_ORDER:
        wait_weights(offset)
    give(1, lambda block: product(block, d_b[...]))
    for block in KEPT:
        put(1, block, product(block, d_b[...]))
    response(0, False)

    scores(1024, lambda t, s: jnp.where(diff >= t * TOK, s, NEG), 2)
    for g in range(4):
        chunk_product(g * 256, g * 256 + 256, False, et, doext.at[2], dvv)
        chunk_product(g * 256, g * 256 + 256, False, dst, qext.at[2], dkk)
        for r in range(2):
            keys = slice(g * 256 + r * TOK, g * 256 + r * TOK + TOK)
            for p in range(2):
                lanes = slice(p * HD, (p + 1) * HD)
                grads[g, r, p, :, :HD] = (dkk[keys, lanes] * SCALE).astype(BF16)
                grads[g, r, p, :, HD:] = dvv[keys, lanes].astype(BF16)
        grads_sibling(g, grads, rc, gsem).start()
    chunk_dq(1024, jnp.full((1, TOK), mine, jnp.int32), kket, dst, d_ap, slice(TOK, 256))
    sums[1].third()
    grads_second(grads, rc, gs, rg, gsem)
    def joint(block):
        value = product(block, d_ap[...])
        offset, side, half = block
        early[offset, half, side] = value[:, TOK:]
        return value[:, :TOK]

    give(0, joint)
    for block in KEPT:
        put(0, block, joint(block))
    sums[1].final()
    sums[1].write(out, 2 * TOK)
    sums[0].second()
    grads_finish(gs, rg, gsem, late)

    def last(block):
        offset, side, half = block
        return early[offset, half, side] + product(block, late[...], 1024)

    give(2, last)
    for block in KEPT:
        put(2, block, last(block))
    sums[0].third()
    sums[2].second()
    sums[0].final()
    sums[0].write(out, TOK)
    sums[2].third()
    sums[2].final()
    sums[2].write(out, 0)
    for g in range(4):
        grads_sibling(g, grads, rc, gsem).wait_send()
    for copy in grads_copies(gs, rg, gsem):
        copy.wait_send()
    for c in range(3):
        sums[c].drain()


def split_kernel(both, out_p, out_r):
    out_p[...] = both[:TOK, :]
    out_r[...] = both[TOK:, :]


def shards(
    q_prompt, k_prompt, v_prompt, do_prompt, q_resp, k_resp, v_resp, do_resp,
    resp_lengths, resp_prompt, w_query, w_key, w_value,
):
    whole = pl.BlockSpec(memory_space=VMEM)
    hbm = pl.BlockSpec(memory_space=pl.ANY)
    scalars = pl.BlockSpec(memory_space=pltpu.SMEM)
    both = pl.pallas_call(
        whole_kernel,
        out_shape=jax.ShapeDtypeStruct((3 * TOK, COLS), BF16),
        in_specs=[scalars] * 2 + [hbm] * 11,
        out_specs=whole,
        scratch_shapes=[
            VMEM((TOK, 1024), BF16),
            VMEM((TOK, 1024), BF16),
            VMEM((256, 1024), BF16),
            VMEM((256, 1024), BF16),
            VMEM((256, HD), BF16),
            VMEM((256, HD), BF16),
            VMEM((WIDE, 256), BF16),
            VMEM((WIDE, 256), BF16),
            VMEM((256, WIDE), BF16),
            VMEM((3, 1024, 256), BF16),
            VMEM((3, 1024, 256), BF16),
            VMEM((WIDE, 256), F32),
            VMEM((WIDE, 256), F32),
            VMEM((WIDE, 256), F32),
            VMEM((WIDE, 256), F32),
            VMEM((WIDE, 1024), BF16),
            VMEM((WIDE, 1024), BF16),
            VMEM((WIDE, 256), F32),
            VMEM((WIDE, 256), F32),
            VMEM((TOK, 256), F32),
            VMEM((256, 256), F32),
            VMEM((TOK, WIDE), BF16),
            VMEM((256, WIDE), BF16),
            VMEM((TOK, 256), BF16),
            VMEM((4, 2, 2, TOK, 256), BF16),
            VMEM((4, 2, 2, HALF, TOK), F32),
            VMEM((4, WIDE, WIDE), BF16),
            VMEM((3, 4, 2, 2, HALF, TOK), BF16),
            VMEM((3, 2, 2, 2, HALF, TOK), BF16),
            VMEM((3, 2, 2, HALF, TOK), BF16),
            VMEM((3, 2, 2, HALF, TOK), BF16),
            VMEM((3, 2, HALF, TOK), BF16),
            VMEM((3, 2, HALF, TOK), BF16),
            VMEM((3, COLS, TOK), F32),
            VMEM((4, 2, TOK, 256), BF16),
            VMEM((4, 2, TOK, 256), BF16),
            VMEM((7, TOK, 256), BF16),
            pltpu.SemaphoreType.DMA((8,)),
            pltpu.SemaphoreType.DMA((7, 2)),
            pltpu.SemaphoreType.DMA((7, 2)),
            pltpu.SemaphoreType.DMA((8, 2)),
            pltpu.SemaphoreType.DMA((8, 2)),
            pltpu.SemaphoreType.DMA((4, 2, 3)),
            pltpu.SemaphoreType.DMA((2, 3, 2, 5, 2)),
            pltpu.SemaphoreType.DMA((2, 11)),
        ],
        compiler_params=pltpu.CompilerParams(
            collective_id=0, has_side_effects=True, vmem_limit_bytes=60 << 20
        ),
        name="attention_back",
    )(
        resp_lengths, resp_prompt, q_prompt, k_prompt, v_prompt, do_prompt,
        q_resp, k_resp, v_resp, do_resp, w_query, w_key, w_value,
    )
    return pl.pallas_call(
        split_kernel,
        out_shape=(
            jax.ShapeDtypeStruct((TOK, COLS), BF16),
            jax.ShapeDtypeStruct((2 * TOK, COLS), BF16),
        ),
        in_specs=[whole],
        out_specs=(whole, whole),
        name="split_rows",
    )(both)


def solution(mesh):
    return jax.shard_map(
        shards,
        mesh=mesh,
        in_specs=(P("seq", "head"),) * 8 + (P("seq", None),) * 2 + (P(None, "head"),) * 3,
        out_specs=(P("seq", "head"), P("seq", "head")),
        check_vma=False,
    )
```

```python
import functools
import math

import jax
import jax.numpy as jnp
from jax import lax
from jax.experimental import pallas as pl
from jax.experimental.pallas import tpu as pltpu
from jax.sharding import PartitionSpec as P

MESH = pl.DeviceIdType.MESH
VMEM = pltpu.VMEM
BF16 = jnp.bfloat16
F32 = jnp.float32
HD = 128
GROUP = 8
TOK = 128
NEG = -1e30
SCALE = 1.0 / math.sqrt(HD)
EXP2 = SCALE * math.log2(math.e)
D = 5120
COLS = 640
HALF = 320
WIDE = 1280
NT = (((1,), (1,)), ((), ()))
NN = (((1,), (0,)), ((), ()))


def dot(a, b, dims):
    return lax.dot_general(a, b, dims, preferred_element_type=F32)


def remote(src, dst, send, recv, seq, head):
    return pltpu.make_async_remote_copy(
        src_ref=src, dst_ref=dst, send_sem=send, recv_sem=recv,
        device_id=(seq, head), device_id_type=MESH,
    )


def seq_place():
    n = lax.axis_index("seq")
    return n // 4, lax.rem(n // 2, 2), lax.rem(n, 2)


def seq_peer(dy, dx):
    y, x, c = seq_place()
    return lax.rem(y + dy + 4, 4) * 4 + lax.rem(x + dx, 2) * 2 + c


def seq_sibling():
    n = lax.axis_index("seq")
    return n + 1 - 2 * lax.rem(n, 2)


SEQ_STEPS = [(0, 1), (1, 0), (3, 0), (2, 0), (1, 1), (3, 1), (2, 1)]


def head_peers():
    h = lax.axis_index("head")
    x, z = h // 4, lax.rem(h, 4)
    base = x * 4
    z1 = base + z + 1 - 2 * lax.rem(z, 2)
    z3 = base + 3 - z
    flip = (1 - x) * 4 + z
    return z1, z3, flip


def key_block(ref, n):
    rows = pl.ds(pl.multiple_of(lax.rem(n, 8) * TOK, TOK), TOK)
    lanes = pl.ds(pl.multiple_of(n // 8 * HD, HD), HD)
    return ref.at[rows, lanes]


def block_pair(keys, n, send, recv, slot, seq):
    head = lax.axis_index("head")
    return [
        remote(key_block(ref, n), key_block(ref, n), send.at[slot, k], recv.at[slot, k], seq, head)
        for k, ref in enumerate(keys)
    ]


def gather_pairs(keys, send, recv, fsend, frecv):
    n = lax.axis_index("seq")
    pairs = []
    for j, (dy, dx) in enumerate(SEQ_STEPS[:4]):
        pairs.append(block_pair(keys, n, send, recv, j, seq_peer(dy, dx)))
    return pairs, block_pair(keys, n, fsend, frecv, 0, seq_sibling())


def gather_start(keys, send, recv, fsend, frecv):
    pairs, own = gather_pairs(keys, send, recv, fsend, frecv)
    for pair in pairs:
        for copy in pair:
            copy.start()
    for copy in own:
        copy.start()


def gather_finish(keys, send, recv, fsend, frecv):
    pairs, own = gather_pairs(keys, send, recv, fsend, frecv)
    partner = seq_peer(0, 1)
    for j, (dy, _) in enumerate(SEQ_STEPS[4:]):
        pairs.append(block_pair(keys, partner, send, recv, 4 + j, seq_peer(dy, 0)))
    forwards = [
        block_pair(keys, seq_peer(-dy, dx), fsend, frecv, j + 1, seq_sibling())
        for j, (dy, dx) in enumerate(SEQ_STEPS)
    ]
    for k in range(2):
        pairs[0][k].wait_recv()
        for pair in pairs[4:]:
            pair[k].start()
    for j in range(7):
        for k in range(2):
            if j > 0:
                pairs[j][k].wait_recv()
            forwards[j][k].start()
    for pair in [own] + forwards:
        for copy in pair:
            copy.wait_recv()
    for pair in pairs + [own] + forwards:
        for copy in pair:
            copy.wait_send()


def segment_of(place, lens_ref):
    end = jnp.int32(0)
    seg = jnp.zeros(place.shape, jnp.int32)
    for c in range(4):
        end = end + lens_ref[0, c]
        seg = seg + (place >= end).astype(jnp.int32)
    return seg


def prompt_of(seg, prompt_ref):
    out = jnp.zeros(seg.shape, jnp.int32)
    for c in range(4):
        out = jnp.where(seg == c, prompt_ref[0, c], out)
    return out


def load_keys(k_r, v_r, kke, vve):
    local = pl.ds(1024, 256)
    kke[local, :HD] = k_r[...]
    kke[local, HD:] = k_r[...]
    vve[local, :HD] = v_r[...]
    vve[local, HD:] = v_r[...]


def turn_keys(kke, kket):
    for r in range(10):
        rows = pl.ds(r * TOK, TOK)
        kket[:, rows] = kke[rows, :].T


def load_rows(q, do, col_prompt, qext, doext):
    first = col_prompt == 0
    zero = jnp.zeros((TOK, HD), BF16)
    first = jnp.broadcast_to(first, (TOK, HD))
    for h in range(GROUP):
        lanes = pl.ds(h * HD, HD)
        rows = pl.ds(h * TOK, TOK)
        qv, dov = q[:, lanes], do[:, lanes]
        qext[rows, :HD] = jnp.where(first, qv, zero)
        qext[rows, HD:] = jnp.where(first, zero, qv)
        doext[rows, :HD] = jnp.where(first, dov, zero)
        doext[rows, HD:] = jnp.where(first, zero, dov)


def fold(x, op):
    return op(x.reshape(x.shape[0] // 8, 8, x.shape[1]), axis=0)


def key_groups(keys):
    size = 256
    return [(k, min(size, keys - k)) for k in range(0, keys, size)]


def chunk_scores(keys, bias_of, qext, doext, kke, vve, s_refs, dp_refs, et, dst):
    low = jnp.full((8, 256), NEG, F32)

    def scores(hp, group, top):
        start, size = group
        s = dot(kke[start : start + size, :], qext[hp * 256 : hp * 256 + 256, :], NT)
        for j in range(0, size, TOK):
            tile = bias_of((start + j) // TOK, s[j : j + TOK])
            s_refs[hp % 2][start + j : start + j + TOK, :] = tile
            top = jnp.maximum(top, fold(tile, jnp.max))
        return top

    def grads(hp, group):
        span = slice(group[0], group[0] + group[1])
        dp_refs[hp % 2][span, :] = dot(vve[span, :], doext[hp * 256 : hp * 256 + 256, :], NT)

    def tiles(group):
        return [slice(j, j + TOK) for j in range(group[0], group[0] + group[1], TOK)]

    groups = key_groups(keys)
    top = low
    for group in groups:
        top = scores(0, group, top)
        grads(0, group)
    for hp in range(4):
        s_ref, dp_ref = s_refs[hp % 2], dp_refs[hp % 2]
        cols = slice(hp * 256, hp * 256 + 256)
        top = jnp.max(top, axis=0, keepdims=True)
        norm = jnp.zeros((8, 256), F32)
        weighted = jnp.zeros((8, 256), F32)
        next_top = low
        for group in groups:
            if hp < 3:
                next_top = scores(hp + 1, group, next_top)
            for span in tiles(group):
                e = jnp.exp2((s_ref[span, :] - top) * EXP2)
                s_ref[span, :] = e
                norm = norm + fold(e, jnp.sum)
                weighted = weighted + fold(e * dp_ref[span, :], jnp.sum)
        inv = 1.0 / jnp.sum(norm, axis=0, keepdims=True)
        mean = jnp.sum(weighted, axis=0, keepdims=True) * inv
        for group in groups:
            if hp < 3:
                grads(hp + 1, group)
            for span in tiles(group):
                p = s_ref[span, :] * inv
                et[span, cols] = p.astype(BF16)
                dst[span, cols] = (p * (dp_ref[span, :] - mean)).astype(BF16)
        top = next_top


def chunk_product(low, high, first, left, right, total):
    for start, size in key_groups(high - low):
        span = slice(low + start, low + start + size)
        value = dot(left[span, :], right[...], NN)
        if first:
            total[span, :] = value
        else:
            total[span, :] += value


def chunk_dq(keys, row_prompt, kket, dst, dq_ref, rows_out):
    first = row_prompt == 0
    for hp in range(4):
        both = dot(kket[:, :keys], dst[:keys, hp * 256 : hp * 256 + 256], NN)
        for k in range(2):
            lanes = slice(k * TOK, (k + 1) * TOK)
            part = jnp.where(first, both[:HD, lanes], both[HD:, lanes]) * SCALE
            h = hp * 2 + k
            dq_ref[rows_out, h * HD : (h + 1) * HD] = part.T.astype(BF16)


SIDES = (
    dict(give=(1, 3), keep=(0, 3), last=1),
    dict(give=(2, 4), keep=(1, 0), last=0),
)


def owner_of(offset, side):
    h = lax.axis_index("head")
    x, z = h // 4, lax.rem(h, 4)
    if offset == 0:
        oz = z
    elif offset == 1:
        oz = z + 1 - 2 * lax.rem(z, 2)
    elif offset == 2:
        oz = lax.rem(z + 2, 4)
    else:
        oz = 3 - z
    ox = x if side == 0 else 1 - x
    return ox * 4 + oz


WEIGHT_ORDER = (2, 1, 3, 0)


def weight_copies(offsets, w_q, w_k, w_v, w, sem):
    for offset in offsets:
        for side in range(2):
            rows = pl.ds(pl.multiple_of(owner_of(offset, side) * COLS, COLS), COLS)
            into = pl.ds(side * COLS, COLS)
            yield from [
                pltpu.make_async_copy(w_q.at[rows], w.at[offset, into, pl.ds(0, 1024)], sem.at[offset, side, 0]),
                pltpu.make_async_copy(w_k.at[rows], w.at[offset, into, pl.ds(1024, HD)], sem.at[offset, side, 1]),
                pltpu.make_async_copy(w_v.at[rows], w.at[offset, into, pl.ds(1152, HD)], sem.at[offset, side, 2]),
            ]


class HeadSum:
    def __init__(self, chunk, pieces, terms, r1, s2, r2, s3, r3, sums, sems):
        self.chunk = chunk
        self.size = HALF // pieces
        self.parts = [(half, piece) for piece in range(pieces) for half in range(2)]
        self.terms, self.r1, self.s2, self.r2, self.s3, self.r3 = (
            terms.at[chunk], r1.at[chunk], s2.at[chunk], r2.at[chunk], s3.at[chunk], r3.at[chunk]
        )
        self.sums = sums.at[chunk]
        self.sems = sems
        self.seq = lax.axis_index("seq")
        self.z1, self.z3, self.flip = head_peers()

    def rows(self, part):
        return pl.ds(part[1] * self.size, self.size)

    def copy(self, part, step):
        half, piece = part
        rows = self.rows(part)
        send, recv = (self.sems.at[k, self.chunk, half, step, piece] for k in range(2))
        near, far = (self.z1, self.z3) if half == 0 else (self.z3, self.z1)
        if step < 2:
            side = 1 - step
            low, high = SIDES[half]["give"]
            src = self.terms.at[pl.ds(low, high - low), half, side, rows]
            return remote(src, self.r1.at[half, side, :, rows], send, recv, self.seq, near)
        if step < 4:
            k = step - 2
            return remote(
                self.s2.at[half, k, rows], self.r2.at[half, k, rows], send, recv, self.seq, self.flip
            )
        return remote(self.s3.at[half, rows], self.r3.at[half, rows], send, recv, self.seq, far)

    def first(self, half, side):
        for part in self.parts:
            if part[0] == half:
                self.copy(part, 1 - side).start()

    def cross(self, part, k):
        half, rows = part[0], self.rows(part)
        offset = SIDES[half]["keep"][k]
        total = self.terms[offset, half, 1, rows].astype(F32) + self.r1[half, 1, k, rows].astype(F32)
        self.s2[half, k, rows] = total.astype(BF16)
        self.copy(part, 2 + k).start()

    def second(self):
        for part in self.parts:
            self.copy(part, 0).wait_recv()
            self.cross(part, SIDES[part[0]]["last"])
        for part in self.parts:
            self.cross(part, 1 - SIDES[part[0]]["last"])

    def kept(self, part, k):
        half, rows = part[0], self.rows(part)
        self.copy(part, 2 + k).wait_recv()
        offset = SIDES[half]["keep"][k]
        return (
            self.terms[offset, half, 0, rows].astype(F32)
            + self.r1[half, 0, k, rows].astype(F32)
            + self.r2[half, k, rows].astype(F32)
        )

    def third(self):
        for part in self.parts:
            self.copy(part, 1).wait_recv()
            total = self.kept(part, SIDES[part[0]]["last"])
            self.s3[part[0], self.rows(part)] = total.astype(BF16)
            self.copy(part, 4).start()

    def final(self):
        for part in self.parts:
            total = self.kept(part, 1 - SIDES[part[0]]["last"])
            self.copy(part, 4).wait_recv()
            start = part[0] * HALF + part[1] * self.size
            self.sums[start : start + self.size, :] = total + self.r3[
                part[0], self.rows(part)
            ].astype(F32)

    def write(self, out, base):
        for part in range(5):
            lanes = slice(part * TOK, (part + 1) * TOK)
            out[base : base + TOK, lanes] = self.sums[lanes, :].T.astype(BF16)

    def drain(self):
        for part in self.parts:
            for step in range(5):
                self.copy(part, step).wait_send()


GIVEN = (
    ((2, 1, 0), (1, 1, 0)), ((2, 1, 1), (3, 1, 1)), ((2, 0, 0), (1, 0, 0)), ((2, 0, 1), (3, 0, 1)),
)
KEPT = (
    (3, 1, 0), (0, 1, 0), (1, 1, 1), (0, 1, 1), (3, 0, 0), (0, 0, 0), (1, 0, 1), (0, 0, 1),
)


def block_rows(side, half):
    start = side * COLS + half * HALF
    return slice(start, start + HALF)


def grads_sibling(group, grads, rc, gsem):
    c = lax.rem(lax.axis_index("seq"), 2)
    return remote(
        grads.at[group, 1 - c], rc.at[group], gsem.at[0, 7 + group], gsem.at[1, 7 + group],
        seq_sibling(), lax.axis_index("head"),
    )


def grads_copies(gs, rg, gsem):
    y, x, c = seq_place()
    copies = []
    for j, (dy, dx) in enumerate(SEQ_STEPS):
        oy = lax.rem(y + dy, 4)
        ox = lax.rem(x + dx, 2)
        block = lax.rem(oy, 2) * 2 + ox
        copies.append(
            remote(
                gs.at[block, oy // 2], rg.at[j], gsem.at[0, j], gsem.at[1, j],
                seq_peer(dy, dx), lax.axis_index("head"),
            )
        )
    return copies


def grads_second(grads, rc, gs, rg, gsem):
    c = lax.rem(lax.axis_index("seq"), 2)
    for b in range(4):
        grads_sibling(b, grads, rc, gsem).wait_recv()
        for p in range(2):
            gs[b, p] = (grads[b, c, p].astype(F32) + rc[b, p].astype(F32)).astype(BF16)
    for copy in grads_copies(gs, rg, gsem):
        copy.start()


def grads_finish(gs, rg, gsem, d_p):
    y, x, c = seq_place()
    total = gs[lax.rem(y, 2) * 2 + x, y // 2].astype(F32)
    for j, copy in enumerate(grads_copies(gs, rg, gsem)):
        copy.wait_recv()
        total = total + rg[j].astype(F32)
    d_p[...] = total.astype(BF16)


def whole_kernel(
    lens_ref, prompt_ref, q_p_h, k_p_h, v_p_h, do_p_h, q_r_h, k_r_h, v_r_h, do_r_h, w_q, w_k, w_v,
    out,
    q_p, do_p, q_r, do_r, k_r, v_r,
    kke, vve, kket, qext, doext, s0, s1, dp0, dp1, et, dst, dkk, dvv, bias0, bias1, d_b, d_ap, late, grads, early,
    w, terms, r1, s2, r2, s3, r3, totals, rc, gs, rg,
    lsem, send, recv, fsend, frecv, wsem, hsem, gsem,
):
    seq, head = lax.axis_index("seq"), lax.axis_index("head")
    barrier = pltpu.get_barrier_semaphore()
    seqs = [seq_sibling()] + [seq_peer(dy, dx) for dy, dx in SEQ_STEPS]
    heads = list(head_peers())
    for peer in seqs:
        pl.semaphore_signal(barrier, inc=1, device_id=(peer, head), device_id_type=MESH)
    for peer in heads:
        pl.semaphore_signal(barrier, inc=1, device_id=(seq, peer), device_id_type=MESH)
    loads = [
        pltpu.make_async_copy(src, dst_ref, lsem.at[k])
        for k, (src, dst_ref) in enumerate((
            (k_p_h, key_block(kke, seq)), (v_p_h, key_block(vve, seq)), (q_r_h, q_r), (do_r_h, do_r),
            (k_r_h, k_r), (v_r_h, v_r), (q_p_h, q_p), (do_p_h, do_p),
        ))
    ]
    for copy in loads:
        copy.start()
    for copy in loads[:2]:
        copy.wait()
    pl.semaphore_wait(barrier, len(seqs) + len(heads))
    gather_start((kke, vve), send, recv, fsend, frecv)
    for copy in weight_copies(WEIGHT_ORDER, w_q, w_k, w_v, w, wsem):
        copy.start()
    for copy in loads[2:]:
        copy.wait()
    sums = [HeadSum(c, (1, 1, 2)[c], terms, r1, s2, r2, s3, r3, totals, hsem) for c in range(3)]
    mine = seq // 8

    row_prompts = []
    for half, bias in ((0, bias0), (1, bias1)):
        base = half * TOK
        col = base + lax.broadcasted_iota(jnp.int32, (TOK, 1), 0)
        row = base + lax.rem(lax.broadcasted_iota(jnp.int32, (1, 256), 1), TOK)
        row_seg = segment_of(row, lens_ref)
        row_prompts.append(prompt_of(row_seg[:, :TOK], prompt_ref))
        key = lax.broadcasted_iota(jnp.int32, (base + TOK, 1), 0)
        key_seg = segment_of(key, lens_ref)
        seen = (key_seg == row_seg) & (key <= row)
        bias[...] = jnp.where(seen, 0.0, NEG)
        span = slice(base, base + TOK)
        load_rows(
            q_r.at[span], do_r.at[span], prompt_of(segment_of(col, lens_ref), prompt_ref),
            qext.at[half], doext.at[half],
        )
    load_rows(q_p, do_p, jnp.full((TOK, 1), mine, jnp.int32), qext.at[2], doext.at[2])
    diff = (
        lax.rem(seq, 8) * TOK
        + lax.rem(lax.broadcasted_iota(jnp.int32, (TOK, 256), 1), TOK)
        - lax.broadcasted_iota(jnp.int32, (TOK, 256), 0)
    )
    d_ap[TOK:, 1024:] = jnp.zeros((TOK, 256), BF16)
    load_keys(k_r, v_r, kke, vve)
    gather_finish((kke, vve), send, recv, fsend, frecv)

    def scores(keys, bias_of, chunk):
        chunk_scores(
            keys, bias_of, qext.at[chunk], doext.at[chunk], kke, vve, (s0, s1), (dp0, dp1), et, dst
        )

    def response(half, first):
        bias = (bias0, bias1)[half]
        keys = 1024 + (half + 1) * TOK

        def local_bias(t, s):
            if t < 8:
                return s
            return s + bias[(t - 8) * TOK : (t - 7) * TOK, :]

        scores(keys, local_bias, half)
        if first:
            turn_keys(kke, kket)
        chunk_product(0, keys, first, et, doext.at[half], dvv)
        chunk_product(0, keys, first, dst, qext.at[half], dkk)
        if not first:
            sums[1].second()
        rows = (d_ap, d_b)[half]
        chunk_dq(keys, row_prompts[half], kket, dst, rows, slice(0, TOK))
        local = slice(1024 + half * TOK, 1024 + half * TOK + TOK)
        rows[:TOK, 1024:1152] = ((dkk[local, :HD] + dkk[local, HD:]) * SCALE).astype(BF16)
        rows[:TOK, 1152:] = (dvv[local, :HD] + dvv[local, HD:]).astype(BF16)

    def wait_weights(offset):
        for copy in weight_copies((offset,), w_q, w_k, w_v, w, wsem):
            copy.wait()

    def product(block, rows, low=0, high=WIDE):
        offset, side, half = block
        return dot(w[offset, block_rows(side, half), low:high], rows, NT)

    def put(chunk, block, value):
        offset, side, half = block
        terms[chunk, offset, half, side] = value.astype(BF16)

    def give(chunk, value_of):
        for pair in GIVEN:
            for block in pair:
                put(chunk, block, value_of(block))
            sums[chunk].first(pair[0][2], pair[0][1])

    response(1, True)
    for offset in WEIGHT_ORDER:
        wait_weights(offset)
    give(1, lambda block: product(block, d_b[...]))
    for block in KEPT:
        put(1, block, product(block, d_b[...]))
    response(0, False)

    scores(1024, lambda t, s: jnp.where(diff >= t * TOK, s, NEG), 2)
    for g in range(4):
        chunk_product(g * 256, g * 256 + 256, False, et, doext.at[2], dvv)
        chunk_product(g * 256, g * 256 + 256, False, dst, qext.at[2], dkk)
        for r in range(2):
            keys = slice(g * 256 + r * TOK, g * 256 + r * TOK + TOK)
            for p in range(2):
                lanes = slice(p * HD, (p + 1) * HD)
                grads[g, r, p, :, :HD] = (dkk[keys, lanes] * SCALE).astype(BF16)
                grads[g, r, p, :, HD:] = dvv[keys, lanes].astype(BF16)
        grads_sibling(g, grads, rc, gsem).start()
    chunk_dq(1024, jnp.full((1, TOK), mine, jnp.int32), kket, dst, d_ap, slice(TOK, 256))
    sums[1].third()
    grads_second(grads, rc, gs, rg, gsem)
    def joint(block):
        value = product(block, d_ap[...])
        offset, side, half = block
        early[offset, half, side] = value[:, TOK:]
        return value[:, :TOK]

    give(0, joint)
    for block in KEPT:
        put(0, block, joint(block))
    sums[0].second()
    sums[1].final()
    sums[1].write(out, 2 * TOK)
    grads_finish(gs, rg, gsem, late)

    def last(block):
        offset, side, half = block
        return early[offset, half, side] + product(block, late[...], 1024)

    give(2, last)
    for block in KEPT:
        put(2, block, last(block))
    sums[0].third()
    sums[2].second()
    sums[0].final()
    sums[0].write(out, TOK)
    sums[2].third()
    sums[2].final()
    sums[2].write(out, 0)
    for g in range(4):
        grads_sibling(g, grads, rc, gsem).wait_send()
    for copy in grads_copies(gs, rg, gsem):
        copy.wait_send()
    for c in range(3):
        sums[c].drain()


def split_kernel(both, out_p, out_r):
    out_p[...] = both[:TOK, :]
    out_r[...] = both[TOK:, :]


def shards(
    q_prompt, k_prompt, v_prompt, do_prompt, q_resp, k_resp, v_resp, do_resp,
    resp_lengths, resp_prompt, w_query, w_key, w_value,
):
    whole = pl.BlockSpec(memory_space=VMEM)
    hbm = pl.BlockSpec(memory_space=pl.ANY)
    scalars = pl.BlockSpec(memory_space=pltpu.SMEM)
    both = pl.pallas_call(
        whole_kernel,
        out_shape=jax.ShapeDtypeStruct((3 * TOK, COLS), BF16),
        in_specs=[scalars] * 2 + [hbm] * 11,
        out_specs=whole,
        scratch_shapes=[
            VMEM((TOK, 1024), BF16),
            VMEM((TOK, 1024), BF16),
            VMEM((256, 1024), BF16),
            VMEM((256, 1024), BF16),
            VMEM((256, HD), BF16),
            VMEM((256, HD), BF16),
            VMEM((WIDE, 256), BF16),
            VMEM((WIDE, 256), BF16),
            VMEM((256, WIDE), BF16),
            VMEM((3, 1024, 256), BF16),
            VMEM((3, 1024, 256), BF16),
            VMEM((WIDE, 256), F32),
            VMEM((WIDE, 256), F32),
            VMEM((WIDE, 256), F32),
            VMEM((WIDE, 256), F32),
            VMEM((WIDE, 1024), BF16),
            VMEM((WIDE, 1024), BF16),
            VMEM((WIDE, 256), F32),
            VMEM((WIDE, 256), F32),
            VMEM((TOK, 256), F32),
            VMEM((256, 256), F32),
            VMEM((TOK, WIDE), BF16),
            VMEM((256, WIDE), BF16),
            VMEM((TOK, 256), BF16),
            VMEM((4, 2, 2, TOK, 256), BF16),
            VMEM((4, 2, 2, HALF, TOK), F32),
            VMEM((4, WIDE, WIDE), BF16),
            VMEM((3, 4, 2, 2, HALF, TOK), BF16),
            VMEM((3, 2, 2, 2, HALF, TOK), BF16),
            VMEM((3, 2, 2, HALF, TOK), BF16),
            VMEM((3, 2, 2, HALF, TOK), BF16),
            VMEM((3, 2, HALF, TOK), BF16),
            VMEM((3, 2, HALF, TOK), BF16),
            VMEM((3, COLS, TOK), F32),
            VMEM((4, 2, TOK, 256), BF16),
            VMEM((4, 2, TOK, 256), BF16),
            VMEM((7, TOK, 256), BF16),
            pltpu.SemaphoreType.DMA((8,)),
            pltpu.SemaphoreType.DMA((7, 2)),
            pltpu.SemaphoreType.DMA((7, 2)),
            pltpu.SemaphoreType.DMA((8, 2)),
            pltpu.SemaphoreType.DMA((8, 2)),
            pltpu.SemaphoreType.DMA((4, 2, 3)),
            pltpu.SemaphoreType.DMA((2, 3, 2, 5, 2)),
            pltpu.SemaphoreType.DMA((2, 11)),
        ],
        compiler_params=pltpu.CompilerParams(
            collective_id=0, has_side_effects=True, vmem_limit_bytes=60 << 20
        ),
        name="attention_back",
    )(
        resp_lengths, resp_prompt, q_prompt, k_prompt, v_prompt, do_prompt,
        q_resp, k_resp, v_resp, do_resp, w_query, w_key, w_value,
    )
    return pl.pallas_call(
        split_kernel,
        out_shape=(
            jax.ShapeDtypeStruct((TOK, COLS), BF16),
            jax.ShapeDtypeStruct((2 * TOK, COLS), BF16),
        ),
        in_specs=[whole],
        out_specs=(whole, whole),
        name="split_rows",
    )(both)


def solution(mesh):
    return jax.shard_map(
        shards,
        mesh=mesh,
        in_specs=(P("seq", "head"),) * 8 + (P("seq", None),) * 2 + (P(None, "head"),) * 3,
        out_specs=(P("seq", "head"), P("seq", "head")),
        check_vma=False,
    )
```
